256 devices in a mesh: lat: 32 (over x, z_lo, core), layer: 8 (over z_hi, y).
Axes of the slice: x: 4, y: 4, z: 8 (z_hi: 2, z_lo: 4; z = z_hi * 4 + z_lo), core: 2. Of those that a mesh axis runs over, the one named last changes fastest.
Arguments:
- streams: bfloat16 [256, 8, 1792], P(None, 'layer'), may hold values from -8 to 8
- enc_weight: bfloat16 [8, 1792, 16384], P('layer', None, 'lat'), may hold values from -0.046875 to 0.046875
- enc_bias: float32 [16384], P('lat'), may hold values from -3 to 3
- dec_weight: bfloat16 [16384, 8, 1792], P('lat', 'layer'), may hold values from -0.125 to 0.125
- dec_bias: float32 [8, 1792], P('layer'), may hold values from -3 to 3
- active: int32 [256, 16384], P(None, 'lat'), may hold values 0 or 1
- bounds: int32 [5], replicated, may hold values from 1 to 16384, as said below
- first_moment: bfloat16 [8, 1792, 16384], P('layer', None, 'lat'), may hold values from -3 to 3
- second_moment: bfloat16 [8, 1792, 16384], P('layer', None, 'lat'), may hold values from 0.049804688 to 2
Outputs:
- new_first: bfloat16 [8, 1792, 16384], P('layer', None, 'lat')
- new_second: bfloat16 [8, 1792, 16384], P('layer', None, 'lat')
- loss_value: float32 [], replicated
- grad_norm: float32 [], replicated
The draws below stay inside these ranges and needn't reach their ends.
Inputs may be any that keep to these rules, and one draw needn't show every extreme that they name: Strictly increasing, the last equal to 16384; latent j lies in prefix k when j < bounds[k].
All inputs are finite; a program needn't handle non-finite values. No bound on the sum of `active` on one device may be relied on, other than what follows from the above.
Results may differ from the reference program's by a relative error of at most 0.002.
Values may be sent and summed in bfloat16 or wider, within the bound.
No kernel may reach another device: no remote copies, remote signals or barrier semaphores. Data moves between devices by JAX's collectives and lax.ppermute only.
A program may use at most 128 MiB of HBM per device.

```python
import math
import jax
import jax.numpy as jnp
from jax import lax

D = 1792
TOKENS = 256
GROUPS = 5
FEATS = 16384
LAYERS = 8


def draw_bounds(key, part):
    key = jax.random.fold_in(key, 7)
    cuts = jax.random.permutation(key, FEATS - 1)[:GROUPS - 1] + 1
    cuts = jnp.sort(cuts.astype(jnp.int32))
    return jnp.concatenate([cuts, jnp.full((1,), FEATS, jnp.int32)]).astype(jnp.int32)


def draw_streams(key, part):
    key = jax.random.fold_in(key, 11)
    token_pos = jnp.arange(TOKENS, dtype=jnp.float32) / max(TOKENS - 1, 1)
    layer_pos = jnp.arange(LAYERS, dtype=jnp.float32) / max(LAYERS - 1, 1)
    scale = 0.4 * jnp.power(3.0, 0.5 * (token_pos[:, None, None] + layer_pos[None, :, None]))
    base = jnp.clip(jax.random.normal(key, (TOKENS, LAYERS, D), jnp.float32), -6.0, 6.0)
    return (base * scale).astype(jnp.bfloat16)


def draw_dec_weight(key, part):
    key = jax.random.fold_in(key, 13)
    latent_pos = jnp.arange(FEATS, dtype=jnp.float32) / max(FEATS - 1, 1)
    scale = jnp.power(3.0, latent_pos)[:, None, None] / (1.8 * FEATS ** 0.5)
    base = jnp.clip(jax.random.normal(key, (FEATS, LAYERS, D), jnp.float32), -5.0, 5.0)
    return (base * scale).astype(jnp.bfloat16)


def with_ends(drawn, own_key, low, high):
    extent = drawn.shape
    place = [jax.random.randint(jax.random.fold_in(own_key, axis), (), 0, extent[axis]) for axis in range(len(extent))]
    drawn = drawn.at[tuple(place)].set(low)
    longest = extent.index(max(extent))
    place[longest] = (place[longest] + 1) % extent[longest]
    return drawn.at[tuple(place)].set(high)


def level_of(stream_key, shape, cuts, smallest, largest):
    level, own = 1.0, jax.random.fold_in(stream_key, 6)
    for position, shards_of in cuts:
        heights = jnp.exp(jax.random.uniform(jax.random.fold_in(own, position), (shards_of,), jnp.float32, smallest / len(cuts), largest / len(cuts)))
        level = level * jnp.repeat(heights, shape[position] // shards_of).reshape([-1 if axis == position else 1 for axis in range(len(shape))])
    return level


def scatter_about(own_key, extent, scale, most, cuts=(), kind=jnp.bfloat16):
    result = jax.random.normal(own_key, extent, jnp.float32) * scale
    if len(cuts) > 0:
        result = level_of(own_key, extent, cuts, -0.22, 0.18) * result
    return jnp.clip(result, min=-most, max=most).astype(kind)


def setup_inputs(seed: int = 0) -> dict:
    seeds = jax.random.split(jax.random.key(seed), 10)
    streams = draw_streams(jax.random.fold_in(seeds[9], 71), 0)
    enc_weight = scatter_about(seeds[1], (LAYERS, D, FEATS), (LAYERS * D) ** -0.5, 0.046875, ((0, 8), (2, 32)))
    enc_bias = scatter_about(seeds[2], (FEATS,), 0.5, 3.0, ((0, 32),), jnp.float32)
    dec_weight = draw_dec_weight(jax.random.fold_in(seeds[9], 71), 0)
    dec_bias = scatter_about(seeds[4], (LAYERS, D), 0.5, 3.0, ((0, 8),), jnp.float32)
    active = with_ends((jax.random.randint(seeds[5], (TOKENS, FEATS), 0, 3) < 1).astype(jnp.int32), jax.random.fold_in(seeds[5], 1), 0, 1)
    bounds = draw_bounds(jax.random.fold_in(seeds[9], 71), 0)
    first_moment = scatter_about(seeds[7], (LAYERS, D, FEATS), 0.5, 3.0, ((0, 8), (2, 32)))
    second_moment = jnp.clip(jnp.exp(math.log(2.0) - 3.6927934 * jax.random.uniform(seeds[8], (LAYERS, D, FEATS), jnp.float32) ** level_of(seeds[8], (LAYERS, D, FEATS), ((0, 8), (2, 32)), -0.2, 0.2)), 0.049804688, 2.0).astype(jnp.bfloat16)
    return dict(streams=streams, enc_weight=enc_weight, enc_bias=enc_bias, dec_weight=dec_weight, dec_bias=dec_bias, active=active, bounds=bounds, first_moment=first_moment, second_moment=second_moment)


def reference(streams, enc_weight, enc_bias, dec_weight, dec_bias, active, bounds, first_moment, second_moment):
    gate_mask = active.astype(jnp.float32)
    flat_in = streams.reshape(TOKENS, LAYERS * D)
    pre_acts = jnp.dot(flat_in, enc_weight.reshape(LAYERS * D, FEATS), preferred_element_type=jnp.float32) + enc_bias
    features = (pre_acts * gate_mask).astype(jnp.bfloat16)
    latent_ids = jnp.arange(FEATS, dtype=jnp.int32)
    prefix_mask = (latent_ids[None, :] < bounds[:, None]).astype(jnp.float32)
    masked = (features[None, :, :] * prefix_mask[:, None, :].astype(jnp.bfloat16)).reshape(GROUPS * TOKENS, FEATS)
    dec_flat = dec_weight.reshape(FEATS, LAYERS * D)
    recon = jnp.dot(masked, dec_flat, preferred_element_type=jnp.float32).reshape(GROUPS, TOKENS, LAYERS, D)
    residuals = recon + dec_bias - streams.astype(jnp.float32)[None]
    loss_value = jnp.sum(residuals * residuals) / (TOKENS * LAYERS * D)
    grad_err = (2.0 * residuals).astype(jnp.bfloat16).reshape(GROUPS * TOKENS, LAYERS * D)
    back = lax.dot_general(grad_err, dec_flat, (((1,), (1,)), ((), ())), preferred_element_type=jnp.float32)
    dfeat = lax.optimization_barrier(jnp.sum(back.reshape(GROUPS, TOKENS, FEATS) * prefix_mask[:, None, :], axis=0))
    dpre = (dfeat * gate_mask).astype(jnp.bfloat16)
    grad_enc = lax.dot_general(flat_in, dpre, (((0,), (0,)), ((), ())), preferred_element_type=jnp.float32)
    grad_enc = grad_enc.reshape(LAYERS, D, FEATS)
    grad_dec = lax.dot_general(masked, grad_err, (((0,), (0,)), ((), ())), preferred_element_type=jnp.float32)
    squares = jnp.sum(grad_enc * grad_enc) + jnp.sum(grad_dec * grad_dec)
    grad_norm = jnp.sqrt(squares)
    limit = math.sqrt(2.0 * LAYERS * D * FEATS)
    factor = limit / jnp.maximum(grad_norm, limit)
    clipped = factor * grad_enc
    new_first = (0.9 * first_moment.astype(jnp.float32) + 0.1 * clipped).astype(jnp.bfloat16)
    new_second = (0.95 * second_moment.astype(jnp.float32) + 0.05 * clipped * clipped).astype(jnp.bfloat16)
    return (new_first, new_second, loss_value, grad_norm)
```

```python
import math

import jax
import jax.numpy as jnp
from jax import lax
from jax.sharding import PartitionSpec as P

BF16 = jnp.bfloat16
F32 = jnp.float32

NX, NZ, NCORE, NHI, NY = 4, 4, 2, 2, 4
X_SETS = [
    [(x * NZ + z) * NCORE + c for x in range(NX)] for z in range(NZ) for c in range(NCORE)
]
Z_SETS = [
    [(x * NZ + z) * NCORE + c for z in range(NZ)] for x in range(NX) for c in range(NCORE)
]
Y_SETS = [[h * NY + y for y in range(NY)] for h in range(NHI)]
CORE_SWAP = [(i, i ^ 1) for i in range(NX * NZ * NCORE)]
HI_SWAP = [(i, i ^ NY) for i in range(NHI * NY)]


def swap_blocks(blocks, axis, sets):
    return lax.all_to_all(blocks, axis, 0, 0, axis_index_groups=sets)


def gather_blocks(block, axis, sets):
    copies = jnp.broadcast_to(block[None], (len(sets[0]), *block.shape))
    return swap_blocks(copies, axis, sets)


def sum_over_layers(partial):
    rows, feats = partial.shape
    parts = partial.astype(BF16).reshape(NY, rows // NY, feats)
    mine = jnp.sum(swap_blocks(parts, "layer", Y_SETS).astype(F32), axis=0)
    return mine + lax.ppermute(mine, "layer", HI_SWAP)


def on_device(
    streams, enc_weight, enc_bias, dec_weight, dec_bias, active, bounds, first_moment, second_moment
):
    lat_count = lax.axis_size("lat")
    layer_count = lax.axis_size("layer")
    lat = lax.axis_index("lat")
    layer = lax.axis_index("layer")
    tokens = streams.shape[0]
    width = streams.shape[2]
    feats_here = enc_weight.shape[2]
    groups = bounds.shape[0]
    core, zlo, xpos = lat % NCORE, (lat // NCORE) % NZ, lat // (NCORE * NZ)
    ypos = layer % NY
    half = tokens // NCORE
    per_x = half // NX
    per_z = per_x // NZ
    quarter = tokens // NY
    layer_in = streams[:, 0, :]
    enc_local = enc_weight[0]
    dec_local = dec_weight[:, 0, :]

    own_in = lax.dynamic_slice_in_dim(layer_in, core * half, half, 0)
    other_in = lax.dynamic_slice_in_dim(layer_in, (1 - core) * half, half, 0)
    turned_in = jnp.concatenate([own_in, other_in], axis=0)
    gate_start = (ypos * quarter + core * half) % tokens
    gate_mask = lax.dynamic_slice_in_dim(active, gate_start, quarter, 0).astype(F32)

    latent_ids = lat * feats_here + lax.iota(jnp.int32, feats_here)
    seg = jnp.sum((bounds[:, None] <= latent_ids[None, :]).astype(jnp.int32), axis=0)
    chip_feats = NCORE * feats_here
    chip_starts = lax.iota(jnp.int32, lat_count // NCORE) * chip_feats
    chip_first = jnp.sum((bounds[:, None] <= chip_starts[None, :]).astype(jnp.int32), axis=0)
    chip_last = jnp.sum(
        (bounds[:, None] <= chip_starts[None, :] + (chip_feats - 1)).astype(jnp.int32), axis=0
    )
    slots_needed = jnp.max(chip_last - chip_first) + 1
    first_here = lax.dynamic_index_in_dim(chip_first, lat // NCORE, 0, keepdims=False)
    first_by_x = lax.dynamic_index_in_dim(chip_first.reshape(NX, NZ), zlo, 1, keepdims=False)

    partial_pre = jnp.dot(turned_in, enc_local, preferred_element_type=F32)
    pre_acts = sum_over_layers(partial_pre) + enc_bias
    features_mine = (pre_acts * gate_mask).astype(BF16)
    features = gather_blocks(features_mine, "layer", Y_SETS).reshape(tokens, feats_here)

    token_start = core * half + xpos * per_x + zlo * per_z
    stream_rows = lax.dynamic_slice_in_dim(layer_in, token_start, per_z, 0).astype(F32)

    def middle(slots, features, dec_local):
        slot_ids = lax.iota(jnp.int32, slots)
        slot_mask = (seg - first_here)[None, :] == slot_ids[:, None]

        def by_slot(rows):
            spread = rows.reshape(NX, 1, per_x, feats_here)
            kept = jnp.where(slot_mask[None, :, None, :], spread, jnp.zeros((), BF16))
            return kept.reshape(NX * slots * per_x, feats_here)

        own_rows = by_slot(features[:half])
        other_rows = by_slot(features[half:])
        theirs = jnp.dot(other_rows, dec_local, preferred_element_type=F32)
        got = lax.ppermute(theirs, "lat", CORE_SWAP)
        ours = jnp.dot(own_rows, dec_local, preferred_element_type=F32)
        chip_sum = (ours + got).astype(BF16).reshape(NX, slots * per_x, width)
        by_x = swap_blocks(chip_sum, "lat", X_SETS).reshape(NX, slots, per_x, width)
        slot_seg = first_by_x[:, None] + slot_ids[None, :]
        sums = []
        for k in range(groups):
            inside = (slot_seg <= k)[:, :, None, None]
            sums.append(jnp.sum(jnp.where(inside, by_x.astype(F32), 0.0), axis=(0, 1)))
        x_sum = jnp.stack(sums).astype(BF16).reshape(groups, NZ, per_z, width)
        by_z = swap_blocks(x_sum.transpose(1, 0, 2, 3), "lat", Z_SETS)
        recon = jnp.sum(by_z.astype(F32), axis=0)
        residuals = recon + dec_bias[0] - stream_rows[None]
        loss = jnp.sum(residuals * residuals)
        grad_err = (2.0 * residuals).astype(BF16).astype(F32)
        suffix = [grad_err[groups - 1]]
        for k in range(groups - 2, -1, -1):
            suffix.append(suffix[-1] + grad_err[k])
        err_sums = jnp.stack(suffix[::-1]).astype(BF16)

        z_rows = gather_blocks(err_sums, "lat", Z_SETS)
        wanted = jnp.minimum(slot_seg, groups - 1)[:, :, None, None, None]
        picked = jnp.broadcast_to(z_rows[None, None, :, 0], (NX, slots, NZ, per_z, width))
        for k in range(1, groups):
            picked = jnp.where(wanted == k, z_rows[None, None, :, k], picked)
        own_err = swap_blocks(picked.reshape(NX, slots * per_x, width), "lat", X_SETS)
        own_err = own_err.reshape(NX * slots * per_x, width)
        other_err = lax.ppermute(own_err, "lat", CORE_SWAP)

        def back(err):
            out = lax.dot_general(
                err, dec_local, (((1,), (1,)), ((), ())), preferred_element_type=F32
            ).reshape(NX, slots, per_x, feats_here)
            return jnp.sum(
                jnp.where(slot_mask[None, :, None, :], out, 0.0), axis=1
            ).reshape(half, feats_here)

        partial_dfeat = jnp.concatenate([back(own_err), back(other_err)], axis=0)
        dfeat = sum_over_layers(partial_dfeat)
        dpre_mine = (dfeat * gate_mask).astype(BF16)
        grad_dec = lax.dot_general(
            jnp.concatenate([own_rows, other_rows], axis=0),
            jnp.concatenate([own_err, other_err], axis=0),
            (((0,), (0,)), ((), ())),
            preferred_element_type=F32,
        )
        return dpre_mine, loss, jnp.sum(grad_dec * grad_dec)

    choices = sorted({min(2, groups), min(3, groups), groups})
    which = sum((slots_needed > c).astype(jnp.int32) for c in choices[:-1])
    dpre_mine, loss_part, dec_squares = lax.switch(
        which,
        [lambda f, d, s=s: middle(s, f, d) for s in choices],
        features,
        dec_local,
    )

    dpre = gather_blocks(dpre_mine, "layer", Y_SETS).reshape(tokens, feats_here)
    grad_enc = lax.dot_general(
        turned_in, dpre, (((0,), (0,)), ((), ())), preferred_element_type=F32
    )
    squares = jnp.sum(grad_enc * grad_enc) + dec_squares
    lanes = lax.iota(jnp.int32, 128)
    row = jnp.where(lanes == 0, squares, jnp.where(lanes == 1, loss_part, 0.0))
    rows = jnp.broadcast_to(row[None], (lat_count * layer_count, 128))
    totals = jnp.sum(lax.all_to_all(rows, ("lat", "layer"), 0, 0), axis=0)
    norm_total, loss_total = totals[0], totals[1]
    grad_norm = jnp.sqrt(norm_total)
    limit = math.sqrt(2.0 * layer_count * width * feats_here * lat_count)
    factor = limit / jnp.maximum(grad_norm, limit)
    clipped = factor * grad_enc[None]
    new_first = (0.9 * first_moment.astype(F32) + 0.1 * clipped).astype(BF16)
    new_second = (0.95 * second_moment.astype(F32) + 0.05 * clipped * clipped).astype(BF16)
    loss_value = loss_total / (tokens * layer_count * width)
    return (new_first, new_second, loss_value, grad_norm)


def solution(mesh):
    in_specs = (
        P(None, "layer", None),
        P("layer", None, "lat"),
        P("lat"),
        P("lat", "layer", None),
        P("layer", None),
        P(None, "lat"),
        P(),
        P("layer", None, "lat"),
        P("layer", None, "lat"),
    )
    out_specs = (P("layer", None, "lat"), P("layer", None, "lat"), P(), P())
    return jax.shard_map(
        on_device, mesh=mesh, in_specs=in_specs, out_specs=out_specs, check_vma=False
    )
```

```python
import functools
import math

import jax
import jax.numpy as jnp
from jax import lax
from jax.experimental import pallas as pl
from jax.experimental.pallas import tpu as pltpu
from jax.sharding import PartitionSpec as P

BF16 = jnp.bfloat16
F32 = jnp.float32

NX, NZ, NCORE, NHI, NY = 4, 4, 2, 2, 4
CHIPS = NX * NZ
PLANE_SETS = [[chip * NCORE + c for chip in range(CHIPS)] for c in range(NCORE)]
Y_SETS = [[h * NY + y for y in range(NY)] for h in range(NHI)]
CORE_SWAP = [(i, i ^ 1) for i in range(NX * NZ * NCORE)]
HI_SWAP = [(i, i ^ NY) for i in range(NHI * NY)]


def swap_blocks(blocks, axis, sets):
    return lax.all_to_all(blocks, axis, 0, 0, axis_index_groups=sets)


def gather_blocks(block, axis, sets):
    copies = jnp.broadcast_to(block[None], (len(sets[0]), *block.shape))
    return swap_blocks(copies, axis, sets)


def sum_over_layers(partial):
    rows, feats = partial.shape
    parts = partial.astype(BF16).reshape(NY, rows // NY, feats)
    mine = jnp.sum(swap_blocks(parts, "layer", Y_SETS).astype(F32), axis=0)
    return mine + lax.ppermute(mine, "layer", HI_SWAP)


def owner_kernel(slots, groups, seg_ref, got_ref, rows_ref, bias_ref, out_ref, loss_ref, sums, errs):
    sums[...] = jnp.zeros_like(sums)
    for c in range(CHIPS):
        for e in range(slots):
            s = seg_ref[c, e]
            sums[s] += got_ref[c, e].astype(F32)
    recon = jnp.zeros_like(rows_ref)
    loss = jnp.zeros_like(rows_ref)
    grad_err = []
    for k in range(groups):
        recon += sums[k]
        residual = recon + bias_ref[...] - rows_ref[...]
        loss += residual * residual
        grad_err.append((2.0 * residual).astype(BF16).astype(F32))
    total = jnp.zeros_like(rows_ref)
    for k in range(groups - 1, -1, -1):
        total += grad_err[k]
        errs[k] = total.astype(BF16)
    loss_ref[0, 0] = jnp.sum(loss)
    for c in range(CHIPS):
        for e in range(slots):
            out_ref[c, e] = errs[seg_ref[c, e]]


def owner_step(slot_seg, got, rows, bias, groups):
    chips, slots, per, width = got.shape
    vmem = pl.BlockSpec(memory_space=pltpu.VMEM)
    smem = pl.BlockSpec(memory_space=pltpu.SMEM)
    return pl.pallas_call(
        functools.partial(owner_kernel, slots, groups),
        out_shape=(
            jax.ShapeDtypeStruct(got.shape, BF16),
            jax.ShapeDtypeStruct((1, 1), F32),
        ),
        in_specs=[smem, vmem, vmem, vmem],
        out_specs=(vmem, smem),
        scratch_shapes=[
            pltpu.VMEM((groups, per, width), F32),
            pltpu.VMEM((groups, per, width), BF16),
        ],
        compiler_params=pltpu.CompilerParams(vmem_limit_bytes=24 * 2**20),
    )(slot_seg, got, rows, bias)


def update_kernel(factor_ref, in_ref, dpre_ref, first_ref, second_ref, new_first_ref, new_second_ref):
    grad = lax.dot_general(
        in_ref[...], dpre_ref[...], (((0,), (0,)), ((), ())), preferred_element_type=F32
    )
    clipped = factor_ref[0, 0] * grad
    new_first_ref[...] = (0.9 * first_ref[...].astype(F32) + 0.1 * clipped).astype(BF16)
    new_second_ref[...] = (
        0.95 * second_ref[...].astype(F32) + 0.05 * clipped * clipped
    ).astype(BF16)


def update(factor, layer_in, dpre, first, second):
    tokens, width = layer_in.shape
    feats = dpre.shape[1]
    tile = 256
    tiles = pl.BlockSpec((tile, feats), lambda i: (i, 0))
    return pl.pallas_call(
        update_kernel,
        grid=(width // tile,),
        out_shape=(jax.ShapeDtypeStruct((width, feats), BF16),) * 2,
        in_specs=[
            pl.BlockSpec(memory_space=pltpu.SMEM),
            pl.BlockSpec((tokens, tile), lambda i: (0, i)),
            pl.BlockSpec((tokens, feats), lambda i: (0, 0)),
            tiles,
            tiles,
        ],
        out_specs=(tiles, tiles),
        compiler_params=pltpu.CompilerParams(vmem_limit_bytes=24 * 2**20),
    )(factor, layer_in, dpre, first, second)


def on_device(
    streams, enc_weight, enc_bias, dec_weight, dec_bias, active, bounds, first_moment, second_moment
):
    lat_count = lax.axis_size("lat")
    layer_count = lax.axis_size("layer")
    lat = lax.axis_index("lat")
    layer = lax.axis_index("layer")
    tokens = streams.shape[0]
    width = streams.shape[2]
    feats_here = enc_weight.shape[2]
    groups = bounds.shape[0]
    core, chip = lat % NCORE, lat // NCORE
    ypos = layer % NY
    half = tokens // NCORE
    per = half // CHIPS
    quarter = tokens // NY
    layer_in = streams[:, 0, :]
    enc_local = enc_weight[0]
    dec_local = dec_weight[:, 0, :]

    own_start, other_start = core * half, (1 - core) * half
    own_in = lax.dynamic_slice_in_dim(layer_in, own_start, half, 0)
    other_in = lax.dynamic_slice_in_dim(layer_in, other_start, half, 0)
    turned_in = jnp.concatenate([own_in, other_in], axis=0)
    gate_mask = lax.dynamic_slice_in_dim(active, ypos * quarter, quarter, 0).astype(F32)
    turned_start = (ypos * quarter + own_start) % tokens
    turned_gate = lax.dynamic_slice_in_dim(active, turned_start, quarter, 0).astype(F32)

    latent_ids = lat * feats_here + lax.iota(jnp.int32, feats_here)
    seg = jnp.sum((bounds[:, None] <= latent_ids[None, :]).astype(jnp.int32), axis=0)
    chip_feats = NCORE * feats_here
    chip_starts = lax.iota(jnp.int32, CHIPS) * chip_feats
    chip_first = jnp.sum((bounds[None, :] <= chip_starts[:, None]).astype(jnp.int32), axis=1)
    chip_last = jnp.sum(
        (bounds[None, :] <= chip_starts[:, None] + (chip_feats - 1)).astype(jnp.int32), axis=1
    )
    slots_needed = jnp.max(chip_last - chip_first) + 1
    first_here = lax.dynamic_index_in_dim(chip_first, chip, 0, keepdims=False)

    partial_pre = jnp.dot(layer_in, enc_local, preferred_element_type=F32)
    pre_acts = sum_over_layers(partial_pre) + enc_bias
    features_mine = (pre_acts * gate_mask).astype(BF16)
    features = gather_blocks(features_mine, "layer", Y_SETS).reshape(tokens, feats_here)

    token_start = own_start + chip * per
    stream_rows = lax.dynamic_slice_in_dim(layer_in, token_start, per, 0).astype(F32)
    own_gram = lax.dot_general(
        turned_in, turned_in, (((1,), (1,)), ((), ())), preferred_element_type=F32
    )

    def middle(slots, features, dec_local):
        slot_ids = lax.iota(jnp.int32, slots)
        slot_mask = (seg - first_here)[None, :] == slot_ids[:, None]

        def by_slot(rows):
            spread = rows.reshape(CHIPS, 1, per, feats_here)
            kept = jnp.where(slot_mask[None, :, None, :], spread, jnp.zeros((), BF16))
            return kept.reshape(CHIPS * slots * per, feats_here)

        own_rows = by_slot(lax.dynamic_slice_in_dim(features, own_start, half, 0))
        other_rows = by_slot(lax.dynamic_slice_in_dim(features, other_start, half, 0))
        theirs = jnp.dot(other_rows, dec_local, preferred_element_type=F32)
        got = lax.ppermute(theirs, "lat", CORE_SWAP)
        ours = jnp.dot(own_rows, dec_local, preferred_element_type=F32)
        chip_sum = (ours + got).astype(BF16).reshape(CHIPS, slots, per, width)
        by_chip = swap_blocks(chip_sum, "lat", PLANE_SETS)
        slot_seg = jnp.minimum(chip_first[:, None] + slot_ids[None, :], groups - 1)
        wanted, loss = owner_step(slot_seg, by_chip, stream_rows, dec_bias, groups)
        own_err = swap_blocks(wanted, "lat", PLANE_SETS).reshape(CHIPS * slots * per, width)
        other_err = lax.ppermute(own_err, "lat", CORE_SWAP)

        def back(err):
            out = lax.dot_general(
                err, dec_local, (((1,), (1,)), ((), ())), preferred_element_type=F32
            ).reshape(CHIPS, slots, per, feats_here)
            return jnp.sum(
                jnp.where(slot_mask[None, :, None, :], out, 0.0), axis=1
            ).reshape(half, feats_here)

        partial_dfeat = jnp.concatenate([back(own_err), back(other_err)], axis=0)
        dfeat = sum_over_layers(partial_dfeat)
        dpre_mine = (dfeat * turned_gate).astype(BF16)
        grad_dec = lax.dot_general(
            jnp.concatenate([own_rows, other_rows], axis=0),
            jnp.concatenate([own_err, other_err], axis=0),
            (((0,), (0,)), ((), ())),
            preferred_element_type=F32,
        )
        return dpre_mine, loss[0, 0], jnp.sum(grad_dec * grad_dec)

    choices = sorted({min(2, groups), min(3, groups), groups})
    which = sum((slots_needed > c).astype(jnp.int32) for c in choices[:-1])
    dpre_mine, loss_part, dec_squares = lax.switch(
        which,
        [lambda f, d, s=s: middle(s, f, d) for s in choices],
        features,
        dec_local,
    )

    dpre = gather_blocks(dpre_mine, "layer", Y_SETS).reshape(tokens, feats_here)
    dpre_gram = lax.dot_general(dpre, dpre, (((1,), (1,)), ((), ())), preferred_element_type=F32)
    squares = jnp.sum(own_gram * dpre_gram) + dec_squares
    lanes = lax.iota(jnp.int32, 128)
    row = jnp.where(lanes == 0, squares, jnp.where(lanes == 1, loss_part, 0.0))
    rows = jnp.broadcast_to(row[None], (lat_count * layer_count, 128))
    totals = jnp.sum(lax.all_to_all(rows, ("lat", "layer"), 0, 0), axis=0)
    norm_total, loss_total = totals[0], totals[1]
    grad_norm = jnp.sqrt(norm_total)
    limit = math.sqrt(2.0 * layer_count * width * feats_here * lat_count)
    factor = limit / jnp.maximum(grad_norm, limit)
    new_first, new_second = update(
        factor.reshape(1, 1), turned_in, dpre, first_moment[0], second_moment[0]
    )
    loss_value = loss_total / (tokens * layer_count * width)
    return (new_first[None], new_second[None], loss_value, grad_norm)


def solution(mesh):
    in_specs = (
        P(None, "layer", None),
        P("layer", None, "lat"),
        P("lat"),
        P("lat", "layer", None),
        P("layer", None),
        P(None, "lat"),
        P(),
        P("layer", None, "lat"),
        P("layer", None, "lat"),
    )
    out_specs = (P("layer", None, "lat"), P("layer", None, "lat"), P(), P())
    return jax.shard_map(
        on_device, mesh=mesh, in_specs=in_specs, out_specs=out_specs, check_vma=False
    )
```

```python
import functools
import math

import jax
import jax.numpy as jnp
from jax import lax
from jax.experimental import pallas as pl
from jax.experimental.pallas import tpu as pltpu
from jax.sharding import PartitionSpec as P

BF16 = jnp.bfloat16
F32 = jnp.float32

NX, NZ, NCORE, NHI, NY = 4, 4, 2, 2, 4
CHIPS = NX * NZ
PLANE_SETS = [[chip * NCORE + c for chip in range(CHIPS)] for c in range(NCORE)]
Y_SETS = [[h * NY + y for y in range(NY)] for h in range(NHI)]
SAME_Y_SETS = [
    [(i * NHI + h) * NY + y for i in range(CHIPS * NCORE) for h in range(NHI)] for y in range(NY)
]
CORE_SWAP = [(i, i ^ 1) for i in range(CHIPS * NCORE)]
HI_SWAP = [(i, i ^ NY) for i in range(NHI * NY)]
Y_SWAPS = [[(i, i ^ m) for i in range(NHI * NY)] for m in (1, 2)]
TAIL = 16


def swap_blocks(blocks, axis, sets):
    return lax.all_to_all(blocks, axis, 0, 0, axis_index_groups=sets)


def vmem_specs(count):
    return [pl.BlockSpec(memory_space=pltpu.VMEM)] * count


SMEM_SPEC = pl.BlockSpec(memory_space=pltpu.SMEM)
SMALL = pltpu.CompilerParams(vmem_limit_bytes=24 * 2**20)
LARGE = pltpu.CompilerParams(vmem_limit_bytes=56 * 2**20)


def pre_kernel(in_ref, enc_ref, out_ref, acc):
    step = pl.program_id(0)
    part = jnp.dot(in_ref[...], enc_ref[...], preferred_element_type=F32)

    @pl.when(step == 0)
    def _():
        acc[...] = part

    @pl.when(step > 0)
    def _():
        acc[...] += part

    @pl.when(step == pl.num_programs(0) - 1)
    def _():
        out_ref[...] = acc[...].astype(BF16)


def partial_pre(layer_in, enc):
    tokens, width = layer_in.shape
    feats = enc.shape[1]
    tile = 256
    return pl.pallas_call(
        pre_kernel,
        grid=(width // tile,),
        out_shape=jax.ShapeDtypeStruct((tokens, feats), BF16),
        in_specs=[
            pl.BlockSpec((tokens, tile), lambda i: (0, i)),
            pl.BlockSpec((tile, feats), lambda i: (i, 0)),
        ],
        out_specs=pl.BlockSpec((tokens, feats), lambda i: (0, 0)),
        scratch_shapes=[pltpu.VMEM((tokens, feats), F32)],
        compiler_params=LARGE,
    )(layer_in, enc)


def feature_kernel(mine_ref, other_ref, bias_ref, gate_ref, out_ref):
    pre = mine_ref[...] + other_ref[...] + bias_ref[...]
    features = (pre * gate_ref[...]).astype(BF16)
    for y in range(NY):
        out_ref[y] = features


def feature_copies(mine, other, bias, gate):
    return pl.pallas_call(
        feature_kernel,
        out_shape=jax.ShapeDtypeStruct((NY, *mine.shape), BF16),
        in_specs=vmem_specs(4),
        out_specs=vmem_specs(1)[0],
        compiler_params=SMALL,
    )(mine, other, bias, gate)


def in_thirds(value, lanes, first):
    whole = jnp.full(lanes.shape, value, F32)
    high = whole.astype(BF16).astype(F32)
    middle = (whole - high).astype(BF16).astype(F32)
    low = whole - high - middle
    rest = jnp.where(lanes == first + 2, low, 0.0)
    rest = jnp.where(lanes == first + 1, middle, rest)
    return jnp.where(lanes == first, high, rest)


def dpre_kernel(mine_ref, other_ref, gate_ref, gram_ref, loss_ref, dec_ref, out_ref):
    dpre = ((mine_ref[...] + other_ref[...]) * gate_ref[...]).astype(BF16)
    pairs = lax.dot_general(dpre, dpre, (((1,), (1,)), ((), ())), preferred_element_type=F32)
    squares = jnp.sum(pairs * gram_ref[...]) + dec_ref[0, 0]
    lanes = lax.broadcasted_iota(jnp.int32, (TAIL, dpre.shape[1]), 1)
    tail = in_thirds(squares, lanes, 0) + in_thirds(loss_ref[0, 0], lanes, 3)
    tokens = dpre.shape[0]
    for y in range(NY):
        out_ref[y, 0:tokens, :] = dpre
        out_ref[y, tokens : tokens + TAIL, :] = tail.astype(BF16)


def dpre_copies(mine, other, gate, gram, loss, dec_squares):
    tokens, feats = mine.shape
    return pl.pallas_call(
        dpre_kernel,
        out_shape=jax.ShapeDtypeStruct((NY, tokens + TAIL, feats), BF16),
        in_specs=vmem_specs(4) + [SMEM_SPEC] * 2,
        out_specs=vmem_specs(1)[0],
        compiler_params=SMALL,
    )(mine, other, gate, gram, loss, dec_squares)


def row_kernel(got_ref, out_ref):
    tokens = got_ref.shape[1] - TAIL
    row = jnp.zeros((TAIL, got_ref.shape[2]), F32)
    for y in range(NY):
        row += got_ref[y, tokens : tokens + TAIL, :].astype(F32)
    out_ref[...] = jnp.broadcast_to(row[0:1][None], out_ref.shape)


def scalar_rows(got, count):
    return pl.pallas_call(
        row_kernel,
        out_shape=jax.ShapeDtypeStruct((count, 1, got.shape[2]), F32),
        in_specs=vmem_specs(1),
        out_specs=vmem_specs(1)[0],
        compiler_params=SMALL,
    )(got)


def grad_kernel(in_ref, got_ref, out_ref):
    tokens = in_ref.shape[0]
    dpre = jnp.concatenate([got_ref[y, 0:tokens, :] for y in range(NY)], axis=1)
    out_ref[...] = lax.dot_general(
        in_ref[...], dpre, (((0,), (0,)), ((), ())), preferred_element_type=F32
    )


def encoder_grad(layer_in, got):
    tokens, width = layer_in.shape
    feats = NY * got.shape[2]
    tile = 256
    return pl.pallas_call(
        grad_kernel,
        grid=(width // tile,),
        out_shape=jax.ShapeDtypeStruct((width, feats), F32),
        in_specs=[
            pl.BlockSpec((tokens, tile), lambda i: (0, i)),
            pl.BlockSpec(got.shape, lambda i: (0, 0, 0)),
        ],
        out_specs=pl.BlockSpec((tile, feats), lambda i: (i, 0)),
        compiler_params=SMALL,
        cost_estimate=pl.CostEstimate(
            flops=2 * tokens * width * feats,
            bytes_accessed=4 * width * feats,
            transcendentals=0,
        ),
    )(layer_in, got)


def owner_kernel(slots, groups, seg_ref, got_ref, rows_ref, bias_ref, out_ref, loss_ref, sums, errs):
    sums[...] = jnp.zeros_like(sums)
    for c in range(CHIPS):
        for e in range(slots):
            s = seg_ref[c, e]
            sums[s] += got_ref[c, e].astype(F32)
    recon = jnp.zeros_like(rows_ref)
    loss = jnp.zeros_like(rows_ref)
    grad_err = []
    for k in range(groups):
        recon += sums[k]
        residual = recon + bias_ref[...] - rows_ref[...]
        loss += residual * residual
        grad_err.append((2.0 * residual).astype(BF16).astype(F32))
    total = jnp.zeros_like(rows_ref)
    for k in range(groups - 1, -1, -1):
        total += grad_err[k]
        errs[k] = total.astype(BF16)
    loss_ref[0, 0] = jnp.sum(loss)
    for c in range(CHIPS):
        for e in range(slots):
            out_ref[c, e] = errs[seg_ref[c, e]]


def owner_step(slot_seg, got, rows, bias, groups):
    chips, slots, per, width = got.shape
    vmem = pl.BlockSpec(memory_space=pltpu.VMEM)
    smem = pl.BlockSpec(memory_space=pltpu.SMEM)
    return pl.pallas_call(
        functools.partial(owner_kernel, slots, groups),
        out_shape=(
            jax.ShapeDtypeStruct(got.shape, BF16),
            jax.ShapeDtypeStruct((1, 1), F32),
        ),
        in_specs=[smem, vmem, vmem, vmem],
        out_specs=(vmem, smem),
        scratch_shapes=[
            pltpu.VMEM((groups, per, width), F32),
            pltpu.VMEM((groups, per, width), BF16),
        ],
        compiler_params=pltpu.CompilerParams(vmem_limit_bytes=24 * 2**20),
    )(slot_seg, got, rows, bias)


def update_kernel(
    limit, loss_scale, rows_ref, grad_ref, first_ref, second_ref,
    new_first_ref, new_second_ref, loss_ref, norm_ref,
):
    totals = jnp.sum(rows_ref[...], axis=0)
    lanes = lax.broadcasted_iota(jnp.int32, totals.shape, 1)
    squares = jnp.sum(jnp.where(lanes < 3, totals, 0.0), axis=1, keepdims=True)
    loss = jnp.sum(jnp.where(lanes < 3, 0.0, totals), axis=1, keepdims=True)
    norm = jnp.sqrt(squares)
    clipped = (limit / jnp.maximum(norm, limit)) * grad_ref[...]
    new_first_ref[...] = (0.9 * first_ref[...].astype(F32) + 0.1 * clipped).astype(BF16)
    new_second_ref[...] = (
        0.95 * second_ref[...].astype(F32) + 0.05 * clipped * clipped
    ).astype(BF16)
    loss_ref[...] = loss * loss_scale
    norm_ref[...] = norm


def update(rows, grad, first, second, limit, loss_scale):
    width, feats = grad.shape
    tile = 256
    tiles = pl.BlockSpec((tile, feats), lambda i: (i, 0))
    one = pl.BlockSpec((1, 1), lambda i: (0, 0))
    return pl.pallas_call(
        functools.partial(update_kernel, limit, loss_scale),
        grid=(width // tile,),
        out_shape=(jax.ShapeDtypeStruct((width, feats), BF16),) * 2
        + (jax.ShapeDtypeStruct((1, 1), F32),) * 2,
        in_specs=[pl.BlockSpec(rows.shape, lambda i: (0, 0, 0)), tiles, tiles, tiles],
        out_specs=(tiles, tiles, one, one),
        compiler_params=LARGE,
    )(rows, grad, first, second)


def on_device(
    streams, enc_weight, enc_bias, dec_weight, dec_bias, active, bounds, first_moment, second_moment
):
    lat_count = lax.axis_size("lat")
    layer_count = lax.axis_size("layer")
    lat = lax.axis_index("lat")
    layer = lax.axis_index("layer")
    tokens = streams.shape[0]
    width = streams.shape[2]
    feats_here = enc_weight.shape[2]
    groups = bounds.shape[0]
    core, chip = lat % NCORE, lat // NCORE
    ypos = layer % NY
    half = tokens // NCORE
    per = half // CHIPS
    quarter = tokens // NY
    layer_in = streams[:, 0, :]
    enc_local = enc_weight[0]
    dec_local = dec_weight[:, 0, :]

    own_start, other_start = core * half, (1 - core) * half
    own_in = lax.dynamic_slice_in_dim(layer_in, own_start, half, 0)
    other_in = lax.dynamic_slice_in_dim(layer_in, other_start, half, 0)
    turned_in = jnp.concatenate([own_in, other_in], axis=0)
    gate = active.astype(F32)
    gate_rows = lax.dynamic_slice_in_dim(gate, ypos * quarter, quarter, 0)
    gate_cols = lax.dynamic_slice_in_dim(gate, ypos * (feats_here // NY), feats_here // NY, 1)
    turned_gate = jnp.concatenate(
        [
            lax.dynamic_slice_in_dim(gate_cols, own_start, half, 0),
            lax.dynamic_slice_in_dim(gate_cols, other_start, half, 0),
        ],
        axis=0,
    )

    latent_ids = lat * feats_here + lax.iota(jnp.int32, feats_here)
    seg = jnp.sum((bounds[:, None] <= latent_ids[None, :]).astype(jnp.int32), axis=0)
    chip_feats = NCORE * feats_here
    chip_starts = lax.iota(jnp.int32, CHIPS) * chip_feats
    chip_first = jnp.sum((bounds[None, :] <= chip_starts[:, None]).astype(jnp.int32), axis=1)
    chip_last = jnp.sum(
        (bounds[None, :] <= chip_starts[:, None] + (chip_feats - 1)).astype(jnp.int32), axis=1
    )
    slots_needed = jnp.max(chip_last - chip_first) + 1
    first_here = lax.dynamic_index_in_dim(chip_first, chip, 0, keepdims=False)

    pre_parts = partial_pre(layer_in, enc_local).reshape(NY, quarter, feats_here)
    pre_mine = jnp.sum(swap_blocks(pre_parts, "layer", Y_SETS).astype(F32), axis=0)
    pre_other = lax.ppermute(pre_mine, "layer", HI_SWAP)
    copies = feature_copies(pre_mine, pre_other, enc_bias[None], gate_rows)
    features = swap_blocks(copies, "layer", Y_SETS).reshape(tokens, feats_here)

    token_start = own_start + chip * per
    stream_rows = lax.dynamic_slice_in_dim(layer_in, token_start, per, 0).astype(F32)
    own_gram = lax.dot_general(
        turned_in, turned_in, (((1,), (1,)), ((), ())), preferred_element_type=F32
    )

    def middle(slots, features, dec_local):
        slot_ids = lax.iota(jnp.int32, slots)
        slot_mask = (seg - first_here)[None, :] == slot_ids[:, None]

        def by_slot(rows):
            spread = rows.reshape(CHIPS, 1, per, feats_here)
            kept = jnp.where(slot_mask[None, :, None, :], spread, jnp.zeros((), BF16))
            return kept.reshape(CHIPS * slots * per, feats_here)

        own_rows = by_slot(lax.dynamic_slice_in_dim(features, own_start, half, 0))
        other_rows = by_slot(lax.dynamic_slice_in_dim(features, other_start, half, 0))
        theirs = jnp.dot(other_rows, dec_local, preferred_element_type=F32)
        got = lax.ppermute(theirs, "lat", CORE_SWAP)
        ours = jnp.dot(own_rows, dec_local, preferred_element_type=F32)
        chip_sum = (ours + got).astype(BF16).reshape(CHIPS, slots, per, width)
        chip_sum, gram = lax.optimization_barrier((chip_sum, own_gram))
        by_chip = swap_blocks(chip_sum, "lat", PLANE_SETS)
        for swap in Y_SWAPS:
            gram = gram + lax.ppermute(gram, "layer", swap)
        slot_seg = jnp.minimum(chip_first[:, None] + slot_ids[None, :], groups - 1)
        wanted, loss = owner_step(slot_seg, by_chip, stream_rows, dec_bias, groups)
        own_err = swap_blocks(wanted, "lat", PLANE_SETS).reshape(CHIPS * slots * per, width)
        other_err = lax.ppermute(own_err, "lat", CORE_SWAP)

        def back(err):
            out = lax.dot_general(
                err, dec_local, (((1,), (1,)), ((), ())), preferred_element_type=F32
            ).reshape(CHIPS, slots, per, feats_here)
            return jnp.sum(
                jnp.where(slot_mask[None, :, None, :], out, 0.0), axis=1
            ).reshape(half, feats_here)

        partial_dfeat = jnp.concatenate([back(own_err), back(other_err)], axis=0)
        parts = partial_dfeat.astype(BF16).reshape(tokens, NY, feats_here // NY).transpose(1, 0, 2)
        mine = jnp.sum(swap_blocks(parts, "layer", Y_SETS).astype(F32), axis=0)
        other = lax.ppermute(mine, "layer", HI_SWAP)
        grad_dec = lax.dot_general(
            jnp.concatenate([own_rows, other_rows], axis=0),
            jnp.concatenate([own_err, other_err], axis=0),
            (((0,), (0,)), ((), ())),
            preferred_element_type=F32,
        )
        dec_squares = jnp.sum(grad_dec * grad_dec).reshape(1, 1)
        return dpre_copies(mine, other, turned_gate, gram, loss, dec_squares)

    choices = sorted({min(2, groups), min(3, groups), groups})
    which = sum((slots_needed > c).astype(jnp.int32) for c in choices[:-1])
    copies = lax.switch(
        which,
        [lambda f, d, s=s: middle(s, f, d) for s in choices],
        features,
        dec_local,
    )
    got = swap_blocks(copies, "layer", Y_SETS)
    rows = scalar_rows(got, len(SAME_Y_SETS[0]))
    rows = lax.all_to_all(rows, ("lat", "layer"), 0, 0, axis_index_groups=SAME_Y_SETS)
    grad_enc = encoder_grad(turned_in, got)
    limit = math.sqrt(2.0 * layer_count * width * feats_here * lat_count)
    new_first, new_second, loss_value, grad_norm = update(
        rows, grad_enc, first_moment[0], second_moment[0],
        limit, 1.0 / (tokens * layer_count * width),
    )
    return (new_first[None], new_second[None], loss_value[0, 0], grad_norm[0, 0])


def solution(mesh):
    in_specs = (
        P(None, "layer", None),
        P("layer", None, "lat"),
        P("lat"),
        P("lat", "layer", None),
        P("layer", None),
        P(None, "lat"),
        P(),
        P("layer", None, "lat"),
        P("layer", None, "lat"),
    )
    out_specs = (P("layer", None, "lat"), P("layer", None, "lat"), P(), P())
    return jax.shard_map(
        on_device, mesh=mesh, in_specs=in_specs, out_specs=out_specs, check_vma=False
    )
```

```python
import functools
import math

import jax
import jax.numpy as jnp
from jax import lax
from jax.experimental import pallas as pl
from jax.experimental.pallas import tpu as pltpu
from jax.sharding import PartitionSpec as P

BF16 = jnp.bfloat16
F32 = jnp.float32

NX, NZ, NCORE, NHI, NY = 4, 4, 2, 2, 4
CHIPS = NX * NZ
PLANE_SETS = [[chip * NCORE + c for chip in range(CHIPS)] for c in range(NCORE)]
Y_SETS = [[h * NY + y for y in range(NY)] for h in range(NHI)]
CORE_SWAP = [(i, i ^ 1) for i in range(CHIPS * NCORE)]
HI_SWAP = [(i, i ^ NY) for i in range(NHI * NY)]
Y_SWAPS = [[(i, i ^ m) for i in range(NHI * NY)] for m in (1, 2)]
LANES = 128
UPDATE_STEPS = 7


def swap_blocks(blocks, axis, sets):
    return lax.all_to_all(blocks, axis, 0, 0, axis_index_groups=sets)


def vmem_specs(count):
    return [pl.BlockSpec(memory_space=pltpu.VMEM)] * count


SMEM_SPEC = pl.BlockSpec(memory_space=pltpu.SMEM)
SMALL = pltpu.CompilerParams(vmem_limit_bytes=24 * 2**20)
LARGE = pltpu.CompilerParams(vmem_limit_bytes=56 * 2**20)


def pre_kernel(in_ref, enc_ref, out_ref, acc):
    step = pl.program_id(0)
    part = jnp.dot(in_ref[...], enc_ref[...], preferred_element_type=F32)

    @pl.when(step == 0)
    def _():
        acc[...] = part

    @pl.when(step > 0)
    def _():
        acc[...] += part

    @pl.when(step == pl.num_programs(0) - 1)
    def _():
        out_ref[...] = acc[...].astype(BF16)


def partial_pre(layer_in, enc):
    tokens, width = layer_in.shape
    feats = enc.shape[1]
    tile = width // 2
    return pl.pallas_call(
        pre_kernel,
        grid=(width // tile,),
        out_shape=jax.ShapeDtypeStruct((tokens, feats), BF16),
        in_specs=[
            pl.BlockSpec((tokens, tile), lambda i: (0, i)),
            pl.BlockSpec((tile, feats), lambda i: (i, 0)),
        ],
        out_specs=pl.BlockSpec((tokens, feats), lambda i: (0, 0)),
        scratch_shapes=[pltpu.VMEM((tokens, feats), F32)],
        compiler_params=LARGE,
    )(layer_in, enc)


def feature_kernel(mine_ref, other_ref, bias_ref, gate_ref, out_ref):
    pre = mine_ref[...] + other_ref[...] + bias_ref[...]
    features = (pre * gate_ref[...]).astype(BF16)
    for y in range(NY):
        out_ref[y] = features


def feature_copies(mine, other, bias, gate):
    return pl.pallas_call(
        feature_kernel,
        out_shape=jax.ShapeDtypeStruct((NY, *mine.shape), BF16),
        in_specs=vmem_specs(4),
        out_specs=vmem_specs(1)[0],
        compiler_params=SMALL,
    )(mine, other, bias, gate)


def parts_kernel(own_ref, other_ref, out_ref):
    half, feats = own_ref.shape
    block = feats // NY
    for y in range(NY):
        out_ref[y, 0:half, :] = own_ref[:, y * block : (y + 1) * block]
        out_ref[y, half : 2 * half, :] = other_ref[:, y * block : (y + 1) * block]


def latent_parts(own, other):
    half, feats = own.shape
    return pl.pallas_call(
        parts_kernel,
        out_shape=jax.ShapeDtypeStruct((NY, NCORE * half, feats // NY), BF16),
        in_specs=vmem_specs(2),
        out_specs=vmem_specs(1)[0],
        compiler_params=SMALL,
    )(own, other)


def dpre_kernel(
    mine_ref, other_ref, gate_ref, gram_ref, loss_ref, dec_ref, out_ref, rows_ref
):
    dpre = ((mine_ref[...] + other_ref[...]) * gate_ref[...]).astype(BF16)
    out_ref[...] = dpre
    pairs = lax.dot_general(dpre, dpre, (((1,), (1,)), ((), ())), preferred_element_type=F32)
    squares = jnp.sum(pairs * gram_ref[...]) + dec_ref[0, 0]
    lanes = lax.broadcasted_iota(jnp.int32, rows_ref.shape, 2)
    rows_ref[...] = jnp.where(lanes == 0, squares, jnp.where(lanes == 1, loss_ref[0, 0], 0.0))


def dpre_and_rows(mine, other, gate, gram, loss, dec_squares, devices):
    return pl.pallas_call(
        dpre_kernel,
        out_shape=(
            jax.ShapeDtypeStruct(mine.shape, BF16),
            jax.ShapeDtypeStruct((devices, 1, LANES), F32),
        ),
        in_specs=vmem_specs(4) + [SMEM_SPEC] * 2,
        out_specs=vmem_specs(2),
        compiler_params=SMALL,
    )(mine, other, gate, gram, loss, dec_squares)


def owner_kernel(
    slots, groups, seg_ref, got_ref, rows_ref, bias_ref, gram_ref, out_ref, loss_ref, sums, errs
):
    sums[...] = jnp.zeros_like(sums)
    for c in range(CHIPS):
        for e in range(slots):
            s = seg_ref[c, e]
            sums[s] += got_ref[c, e].astype(F32)
    recon = jnp.zeros_like(rows_ref)
    loss = jnp.zeros_like(rows_ref)
    grad_err = []
    for k in range(groups):
        recon += sums[k]
        residual = recon + bias_ref[...] - rows_ref[...]
        loss += residual * residual
        grad_err.append((2.0 * residual).astype(BF16).astype(F32))
    total = jnp.zeros_like(rows_ref)
    for k in range(groups - 1, -1, -1):
        total += grad_err[k]
        errs[k] = total.astype(BF16)
    loss_ref[0, 0] = jnp.sum(loss)
    for c in range(CHIPS):
        for e in range(slots):
            out_ref[c, e] = errs[seg_ref[c, e]]


def owner_step(slot_seg, got, rows, bias, gram, groups):
    chips, slots, per, width = got.shape
    vmem = pl.BlockSpec(memory_space=pltpu.VMEM)
    smem = pl.BlockSpec(memory_space=pltpu.SMEM)
    return pl.pallas_call(
        functools.partial(owner_kernel, slots, groups),
        out_shape=(
            jax.ShapeDtypeStruct(got.shape, BF16),
            jax.ShapeDtypeStruct((1, 1), F32),
        ),
        in_specs=[smem, vmem, vmem, vmem, pl.BlockSpec(memory_space=pl.ANY)],
        out_specs=(vmem, smem),
        scratch_shapes=[
            pltpu.VMEM((groups, per, width), F32),
            pltpu.VMEM((groups, per, width), BF16),
        ],
        compiler_params=pltpu.CompilerParams(vmem_limit_bytes=24 * 2**20),
    )(slot_seg, got, rows, bias, gram)


def update_kernel(
    limit, loss_scale, ypos_ref, rows_ref, in_ref, near_ref, far_ref, first_hbm, second_hbm,
    new_first_hbm, new_second_hbm, loss_ref, norm_ref,
    dpre, first, second, new_first, new_second, sems,
):
    width = in_ref.shape[1]
    tile = width // UPDATE_STEPS
    block = near_ref.shape[2]

    def copies(i):
        here = pl.ds(i * tile, tile)
        pairs = (
            (first_hbm, first), (second_hbm, second),
            (new_first, new_first_hbm), (new_second, new_second_hbm),
        )
        return [
            pltpu.make_async_copy(src.at[here, :], dst.at[here, :], sems.at[n, i])
            for n, (src, dst) in enumerate(pairs)
        ]

    steps = [copies(i) for i in range(UPDATE_STEPS)]
    for step in steps:
        step[0].start()
        step[1].start()
    for at, ref in ((0, near_ref), (2, far_ref)):
        for b in range(2):
            owner = ypos_ref[0, 0] ^ (at + b)
            dpre[:, pl.ds(pl.multiple_of(owner * block, block), block)] = ref[b]
    totals = jnp.sum(rows_ref[...], axis=0)
    lanes = lax.broadcasted_iota(jnp.int32, totals.shape, 1)
    squares = jnp.sum(jnp.where(lanes == 0, totals, 0.0), axis=1, keepdims=True)
    loss = jnp.sum(jnp.where(lanes == 1, totals, 0.0), axis=1, keepdims=True)
    norm = jnp.sqrt(squares)
    factor = limit / jnp.maximum(norm, limit)
    loss_ref[...] = loss * loss_scale
    norm_ref[...] = norm
    for i, step in enumerate(steps):
        here = slice(i * tile, (i + 1) * tile)
        grad = lax.dot_general(
            in_ref[:, here], dpre[...], (((0,), (0,)), ((), ())), preferred_element_type=F32
        )
        clipped = factor * grad
        step[0].wait()
        new_first[here, :] = (0.9 * first[here, :].astype(F32) + 0.1 * clipped).astype(BF16)
        step[2].start()
        step[1].wait()
        new_second[here, :] = (
            0.95 * second[here, :].astype(F32) + 0.05 * clipped * clipped
        ).astype(BF16)
        step[3].start()
    for step in steps:
        step[2].wait()
        step[3].wait()


def update(ypos, rows, layer_in, near, far, first, second, limit, loss_scale):
    width, feats = first.shape
    tokens = layer_in.shape[0]
    hbm = pl.BlockSpec(memory_space=pl.ANY)
    whole = pltpu.VMEM((width, feats), BF16)
    return pl.pallas_call(
        functools.partial(update_kernel, limit, loss_scale),
        out_shape=(jax.ShapeDtypeStruct((width, feats), BF16),) * 2
        + (jax.ShapeDtypeStruct((1, 1), F32),) * 2,
        in_specs=[SMEM_SPEC] + vmem_specs(4) + [hbm] * 2,
        out_specs=[hbm] * 2 + vmem_specs(2),
        scratch_shapes=[
            pltpu.VMEM((tokens, feats), BF16), whole, whole, whole, whole,
            pltpu.SemaphoreType.DMA((4, UPDATE_STEPS)),
        ],
        compiler_params=SMALL,
    )(ypos, rows, layer_in, near, far, first, second)


def on_device(
    streams, enc_weight, enc_bias, dec_weight, dec_bias, active, bounds, first_moment, second_moment
):
    lat_count = lax.axis_size("lat")
    layer_count = lax.axis_size("layer")
    lat = lax.axis_index("lat")
    layer = lax.axis_index("layer")
    tokens = streams.shape[0]
    width = streams.shape[2]
    feats_here = enc_weight.shape[2]
    groups = bounds.shape[0]
    core, chip = lat % NCORE, lat // NCORE
    ypos = layer % NY
    half = tokens // NCORE
    per = half // CHIPS
    quarter = tokens // NY
    layer_in = streams[:, 0, :]
    enc_local = enc_weight[0]
    dec_local = dec_weight[:, 0, :]

    own_start, other_start = core * half, (1 - core) * half
    own_in = lax.dynamic_slice_in_dim(layer_in, own_start, half, 0)
    other_in = lax.dynamic_slice_in_dim(layer_in, other_start, half, 0)
    turned_in = jnp.concatenate([own_in, other_in], axis=0)
    gate = active.astype(F32)
    gate_rows = lax.dynamic_slice_in_dim(gate, ypos * quarter, quarter, 0)
    gate_cols = lax.dynamic_slice_in_dim(gate, ypos * (feats_here // NY), feats_here // NY, 1)
    turned_gate = jnp.concatenate(
        [
            lax.dynamic_slice_in_dim(gate_cols, own_start, half, 0),
            lax.dynamic_slice_in_dim(gate_cols, other_start, half, 0),
        ],
        axis=0,
    )

    latent_ids = lat * feats_here + lax.iota(jnp.int32, feats_here)
    seg = jnp.sum((bounds[:, None] <= latent_ids[None, :]).astype(jnp.int32), axis=0)
    chip_feats = NCORE * feats_here
    chip_starts = lax.iota(jnp.int32, CHIPS) * chip_feats
    chip_first = jnp.sum((bounds[None, :] <= chip_starts[:, None]).astype(jnp.int32), axis=1)
    chip_last = jnp.sum(
        (bounds[None, :] <= chip_starts[:, None] + (chip_feats - 1)).astype(jnp.int32), axis=1
    )
    slots_needed = jnp.max(chip_last - chip_first) + 1
    first_here = lax.dynamic_index_in_dim(chip_first, chip, 0, keepdims=False)
    slot_here = lax.optimization_barrier(seg - first_here)

    pre_parts = partial_pre(layer_in, enc_local).reshape(NY, quarter, feats_here)
    pre_mine = jnp.sum(swap_blocks(pre_parts, "layer", Y_SETS).astype(F32), axis=0)
    pre_other = lax.ppermute(pre_mine, "layer", HI_SWAP)
    copies = feature_copies(pre_mine, pre_other, enc_bias[None], gate_rows)
    features = swap_blocks(copies, "layer", Y_SETS).reshape(tokens, feats_here)

    token_start = own_start + chip * per
    stream_rows = lax.dynamic_slice_in_dim(layer_in, token_start, per, 0).astype(F32)
    def middle(slots, features, dec_local):
        slot_ids = lax.iota(jnp.int32, slots)
        slot_mask = slot_here[None, :] == slot_ids[:, None]

        def by_slot(rows):
            spread = rows.reshape(CHIPS, 1, per, feats_here)
            kept = jnp.where(slot_mask[None, :, None, :], spread, jnp.zeros((), BF16))
            return kept.reshape(CHIPS * slots * per, feats_here)

        own_rows = by_slot(lax.dynamic_slice_in_dim(features, own_start, half, 0))
        other_rows = by_slot(lax.dynamic_slice_in_dim(features, other_start, half, 0))
        theirs = jnp.dot(other_rows, dec_local, preferred_element_type=F32).astype(BF16)
        got = lax.ppermute(theirs, "lat", CORE_SWAP).astype(F32)
        ours = jnp.dot(own_rows, dec_local, preferred_element_type=F32)
        chip_sum = (ours + got).astype(BF16).reshape(CHIPS, slots, per, width)
        chip_sum, turned = lax.optimization_barrier((chip_sum, turned_in))
        by_chip = swap_blocks(chip_sum, "lat", PLANE_SETS)
        gram = lax.dot_general(
            turned, turned, (((1,), (1,)), ((), ())), preferred_element_type=F32
        )
        for swap in Y_SWAPS:
            gram = gram + lax.ppermute(gram, "layer", swap)
        slot_seg = jnp.minimum(chip_first[:, None] + slot_ids[None, :], groups - 1)
        wanted, loss = owner_step(slot_seg, by_chip, stream_rows, dec_bias, gram, groups)
        own_err = swap_blocks(wanted, "lat", PLANE_SETS).reshape(CHIPS * slots * per, width)
        other_err = lax.ppermute(own_err, "lat", CORE_SWAP)


        def back(err):
            out = lax.dot_general(
                err, dec_local, (((1,), (1,)), ((), ())), preferred_element_type=F32
            ).reshape(CHIPS, slots, per, feats_here)
            kept = jnp.where(slot_mask[None, :, None, :], out, 0.0)
            return jnp.sum(kept, axis=1).astype(BF16).reshape(half, feats_here)

        parts = latent_parts(back(own_err), back(other_err))
        pairs = [
            lax.dot_general(r, r, (((1,), (1,)), ((), ())), preferred_element_type=F32)
            for r in (
                jnp.concatenate([own_rows, other_rows], axis=0),
                jnp.concatenate([own_err, other_err], axis=0),
            )
        ]
        dec_squares = jnp.sum(pairs[0] * pairs[1]).reshape(1, 1)
        return parts, gram, loss, dec_squares

    choices = sorted({min(2, groups), min(3, groups), groups})
    which = sum((slots_needed > c).astype(jnp.int32) for c in choices[:-1])
    parts, gram, loss, dec_squares = lax.switch(
        which, [functools.partial(middle, s) for s in choices], features, dec_local
    )
    mine = jnp.sum(swap_blocks(parts, "layer", Y_SETS).astype(F32), axis=0)
    other = lax.ppermute(mine, "layer", HI_SWAP)
    dpre, rows = dpre_and_rows(
        mine, other, turned_gate, gram, loss, dec_squares, lat_count * layer_count
    )
    rows = lax.all_to_all(rows, ("lat", "layer"), 0, 0)
    near = jnp.stack([dpre, lax.ppermute(dpre, "layer", Y_SWAPS[0])])
    far = lax.ppermute(near, "layer", Y_SWAPS[1])
    limit = math.sqrt(2.0 * layer_count * width * feats_here * lat_count)
    new_first, new_second, loss_value, grad_norm = update(
        ypos.reshape(1, 1), rows, turned_in, near, far, first_moment[0], second_moment[0],
        limit, 1.0 / (tokens * layer_count * width),
    )
    return (new_first[None], new_second[None], loss_value[0, 0], grad_norm[0, 0])


def solution(mesh):
    in_specs = (
        P(None, "layer", None),
        P("layer", None, "lat"),
        P("lat"),
        P("lat", "layer", None),
        P("layer", None),
        P(None, "lat"),
        P(),
        P("layer", None, "lat"),
        P("layer", None, "lat"),
    )
    out_specs = (P("layer", None, "lat"), P("layer", None, "lat"), P(), P())
    return jax.shard_map(
        on_device, mesh=mesh, in_specs=in_specs, out_specs=out_specs, check_vma=False
    )
```

```python
import functools
import math

import jax
import jax.numpy as jnp
from jax import lax
from jax.experimental import pallas as pl
from jax.experimental.pallas import tpu as pltpu
from jax.sharding import PartitionSpec as P

BF16 = jnp.bfloat16
F32 = jnp.float32

NX, NZ, NCORE, NHI, NY = 4, 4, 2, 2, 4
CHIPS = NX * NZ
PLANE_SETS = [[chip * NCORE + c for chip in range(CHIPS)] for c in range(NCORE)]
Y_SETS = [[h * NY + y for y in range(NY)] for h in range(NHI)]
CORE_SWAP = [(i, i ^ 1) for i in range(CHIPS * NCORE)]
HI_SWAP = [(i, i ^ NY) for i in range(NHI * NY)]
Y_SWAPS = [[(i, i ^ m) for i in range(NHI * NY)] for m in (1, 2)]
LANES = 128
UPDATE_STEPS = 7


def swap_blocks(blocks, axis, sets):
    return lax.all_to_all(blocks, axis, 0, 0, axis_index_groups=sets)


def vmem_specs(count):
    return [pl.BlockSpec(memory_space=pltpu.VMEM)] * count


SMEM_SPEC = pl.BlockSpec(memory_space=pltpu.SMEM)
SMALL = pltpu.CompilerParams(vmem_limit_bytes=10 * 2**20)
LARGE = pltpu.CompilerParams(vmem_limit_bytes=56 * 2**20)


def pre_kernel(in_ref, enc_ref, out_ref, acc):
    step = pl.program_id(0)
    part = jnp.dot(in_ref[...], enc_ref[...], preferred_element_type=F32)

    @pl.when(step == 0)
    def _():
        acc[...] = part

    @pl.when(step > 0)
    def _():
        acc[...] += part

    @pl.when(step == pl.num_programs(0) - 1)
    def _():
        out_ref[...] = acc[...].astype(BF16)


def partial_pre(layer_in, enc):
    tokens, width = layer_in.shape
    feats = enc.shape[1]
    tile = width // 2
    return pl.pallas_call(
        pre_kernel,
        grid=(width // tile,),
        out_shape=jax.ShapeDtypeStruct((tokens, feats), BF16),
        in_specs=[
            pl.BlockSpec((tokens, tile), lambda i: (0, i)),
            pl.BlockSpec((tile, feats), lambda i: (i, 0)),
        ],
        out_specs=pl.BlockSpec((tokens, feats), lambda i: (0, 0)),
        scratch_shapes=[pltpu.VMEM((tokens, feats), F32)],
        compiler_params=LARGE,
    )(layer_in, enc)


def feature_kernel(mine_ref, other_ref, bias_ref, gate_ref, out_ref):
    pre = mine_ref[...] + other_ref[...] + bias_ref[...]
    features = (pre * gate_ref[...]).astype(BF16)
    for y in range(NY):
        out_ref[y] = features


def feature_copies(mine, other, bias, gate):
    return pl.pallas_call(
        feature_kernel,
        out_shape=jax.ShapeDtypeStruct((NY, *mine.shape), BF16),
        in_specs=vmem_specs(4),
        out_specs=vmem_specs(1)[0],
        compiler_params=SMALL,
    )(mine, other, bias, gate)


def parts_kernel(own_ref, other_ref, out_ref):
    half, feats = own_ref.shape
    block = feats // NY
    for y in range(NY):
        out_ref[y, 0:half, :] = own_ref[:, y * block : (y + 1) * block]
        out_ref[y, half : 2 * half, :] = other_ref[:, y * block : (y + 1) * block]


def latent_parts(own, other):
    half, feats = own.shape
    return pl.pallas_call(
        parts_kernel,
        out_shape=jax.ShapeDtypeStruct((NY, NCORE * half, feats // NY), BF16),
        in_specs=vmem_specs(2),
        out_specs=vmem_specs(1)[0],
        compiler_params=SMALL,
    )(own, other)


def dpre_kernel(
    mine_ref, other_ref, gate_ref, scalars_ref, gram_hbm, out_ref, rows_ref, gram, sem
):
    copy = pltpu.make_async_copy(gram_hbm, gram, sem)
    copy.start()
    dpre = ((mine_ref[...] + other_ref[...]) * gate_ref[...]).astype(BF16)
    out_ref[...] = dpre
    pairs = lax.dot_general(dpre, dpre, (((1,), (1,)), ((), ())), preferred_element_type=F32)
    copy.wait()
    squares = jnp.sum(pairs * gram[...])
    lanes = lax.broadcasted_iota(jnp.int32, (1, LANES), 1)
    row = scalars_ref[0:1, :] + jnp.where(lanes == 0, squares, 0.0)
    rows_ref[...] = jnp.broadcast_to(row[None], rows_ref.shape)


def dpre_and_rows(mine, other, gate, scalars, gram, devices):
    return pl.pallas_call(
        dpre_kernel,
        out_shape=(
            jax.ShapeDtypeStruct(mine.shape, BF16),
            jax.ShapeDtypeStruct((devices, 1, LANES), F32),
        ),
        in_specs=vmem_specs(4) + [pl.BlockSpec(memory_space=pl.ANY)],
        out_specs=vmem_specs(2),
        scratch_shapes=[pltpu.VMEM(gram.shape, F32), pltpu.SemaphoreType.DMA],
        compiler_params=SMALL,
    )(mine, other, gate, scalars, gram)


def owner_kernel(
    slots, groups, seg_ref, got_ref, rows_ref, bias_ref, near_ref, far_ref,
    out_ref, loss_ref, gram_hbm, sums, errs, gram, sem,
):
    gram[...] = near_ref[...] + far_ref[...]
    copy = pltpu.make_async_copy(gram, gram_hbm, sem)
    copy.start()
    sums[...] = jnp.zeros_like(sums)
    for c in range(CHIPS):
        for e in range(slots):
            s = seg_ref[c, e]
            sums[s] += got_ref[c, e].astype(F32)
    recon = jnp.zeros_like(rows_ref)
    loss = jnp.zeros_like(rows_ref)
    grad_err = []
    for k in range(groups):
        recon += sums[k]
        residual = recon + bias_ref[...] - rows_ref[...]
        loss += residual * residual
        grad_err.append((2.0 * residual).astype(BF16).astype(F32))
    total = jnp.zeros_like(rows_ref)
    for k in range(groups - 1, -1, -1):
        total += grad_err[k]
        errs[k] = total.astype(BF16)
    loss_ref[0, 0] = jnp.sum(loss)
    for c in range(CHIPS):
        for e in range(slots):
            out_ref[c, e] = errs[seg_ref[c, e]]
    copy.wait()


def owner_step(slot_seg, got, rows, bias, near_gram, far_gram, groups):
    chips, slots, per, width = got.shape
    vmem = pl.BlockSpec(memory_space=pltpu.VMEM)
    smem = pl.BlockSpec(memory_space=pltpu.SMEM)
    return pl.pallas_call(
        functools.partial(owner_kernel, slots, groups),
        out_shape=(
            jax.ShapeDtypeStruct(got.shape, BF16),
            jax.ShapeDtypeStruct((1, 1), F32),
            jax.ShapeDtypeStruct(near_gram.shape, F32),
        ),
        in_specs=[smem, vmem, vmem, vmem, vmem, vmem],
        out_specs=(vmem, smem, pl.BlockSpec(memory_space=pl.ANY)),
        scratch_shapes=[
            pltpu.VMEM((groups, per, width), F32),
            pltpu.VMEM((groups, per, width), BF16),
            pltpu.VMEM(near_gram.shape, F32),
            pltpu.SemaphoreType.DMA,
        ],
        compiler_params=SMALL,
    )(slot_seg, got, rows, bias, near_gram, far_gram)


def update_kernel(
    limit, loss_scale, ypos_ref, rows_ref, in_ref, near_ref, far_ref, first, second,
    new_first_hbm, new_second_hbm, loss_ref, norm_ref,
    dpre, new_first, new_second, sems,
):
    width = in_ref.shape[1]
    tile = width // UPDATE_STEPS
    block = near_ref.shape[2]
    for at, ref in ((0, near_ref), (2, far_ref)):
        for b in range(2):
            owner = ypos_ref[0, 0] ^ (at + b)
            dpre[:, pl.ds(pl.multiple_of(owner * block, block), block)] = ref[b]
    totals = jnp.sum(rows_ref[...], axis=0)
    lanes = lax.broadcasted_iota(jnp.int32, totals.shape, 1)
    squares = jnp.sum(jnp.where(lanes == 0, totals, 0.0), axis=1, keepdims=True)
    loss = jnp.sum(jnp.where(lanes == 1, totals, 0.0), axis=1, keepdims=True)
    norm = jnp.sqrt(squares)
    factor = limit / jnp.maximum(norm, limit)
    loss_ref[...] = loss * loss_scale
    norm_ref[...] = norm
    copies = []
    for i in range(UPDATE_STEPS):
        here = slice(i * tile, (i + 1) * tile)
        rows = pl.ds(i * tile, tile)
        grad = lax.dot_general(
            in_ref[:, here], dpre[...], (((0,), (0,)), ((), ())), preferred_element_type=F32
        )
        clipped = factor * grad
        new_first[here, :] = (0.9 * first[here, :].astype(F32) + 0.1 * clipped).astype(BF16)
        new_second[here, :] = (
            0.95 * second[here, :].astype(F32) + 0.05 * clipped * clipped
        ).astype(BF16)
        for n, (src, dst) in enumerate(
            ((new_first, new_first_hbm), (new_second, new_second_hbm))
        ):
            copy = pltpu.make_async_copy(src.at[rows, :], dst.at[rows, :], sems.at[n, i])
            copy.start()
            copies.append(copy)
    for copy in copies:
        copy.wait()


def update(ypos, rows, layer_in, near, far, first, second, limit, loss_scale):
    width, feats = first.shape
    tokens = layer_in.shape[0]
    hbm = pl.BlockSpec(memory_space=pl.ANY)
    whole = pltpu.VMEM((width, feats), BF16)
    return pl.pallas_call(
        functools.partial(update_kernel, limit, loss_scale),
        out_shape=(jax.ShapeDtypeStruct((width, feats), BF16),) * 2
        + (jax.ShapeDtypeStruct((1, 1), F32),) * 2,
        in_specs=[SMEM_SPEC] + vmem_specs(6),
        out_specs=[hbm] * 2 + vmem_specs(2),
        scratch_shapes=[
            pltpu.VMEM((tokens, feats), BF16), whole, whole,
            pltpu.SemaphoreType.DMA((2, UPDATE_STEPS)),
        ],
        compiler_params=pltpu.CompilerParams(vmem_limit_bytes=13 * 2**20),
    )(ypos, rows, layer_in, near, far, first, second)


def on_device(
    streams, enc_weight, enc_bias, dec_weight, dec_bias, active, bounds, first_moment, second_moment
):
    lat_count = lax.axis_size("lat")
    layer_count = lax.axis_size("layer")
    lat = lax.axis_index("lat")
    layer = lax.axis_index("layer")
    tokens = streams.shape[0]
    width = streams.shape[2]
    feats_here = enc_weight.shape[2]
    groups = bounds.shape[0]
    core, chip = lat % NCORE, lat // NCORE
    ypos = layer % NY
    half = tokens // NCORE
    per = half // CHIPS
    quarter = tokens // NY
    layer_in = streams[:, 0, :]
    enc_local = enc_weight[0]
    dec_local = dec_weight[:, 0, :]

    own_start, other_start = core * half, (1 - core) * half
    own_in = lax.dynamic_slice_in_dim(layer_in, own_start, half, 0)
    other_in = lax.dynamic_slice_in_dim(layer_in, other_start, half, 0)
    turned_in = jnp.concatenate([own_in, other_in], axis=0)
    gate = active.astype(F32)
    gate_rows = lax.dynamic_slice_in_dim(gate, ypos * quarter, quarter, 0)
    gate_cols = lax.dynamic_slice_in_dim(gate, ypos * (feats_here // NY), feats_here // NY, 1)
    turned_gate = jnp.concatenate(
        [
            lax.dynamic_slice_in_dim(gate_cols, own_start, half, 0),
            lax.dynamic_slice_in_dim(gate_cols, other_start, half, 0),
        ],
        axis=0,
    )

    latent_ids = lat * feats_here + lax.iota(jnp.int32, feats_here)
    seg = jnp.sum((bounds[:, None] <= latent_ids[None, :]).astype(jnp.int32), axis=0)
    chip_feats = NCORE * feats_here
    chip_starts = lax.iota(jnp.int32, CHIPS) * chip_feats
    chip_first = jnp.sum((bounds[None, :] <= chip_starts[:, None]).astype(jnp.int32), axis=1)
    chip_last = jnp.sum(
        (bounds[None, :] <= chip_starts[:, None] + (chip_feats - 1)).astype(jnp.int32), axis=1
    )
    slots_needed = jnp.max(chip_last - chip_first) + 1
    first_here = lax.dynamic_index_in_dim(chip_first, chip, 0, keepdims=False)
    slot_here = lax.optimization_barrier(seg - first_here)

    pre_parts = partial_pre(layer_in, enc_local).reshape(NY, quarter, feats_here)
    pre_mine = jnp.sum(swap_blocks(pre_parts, "layer", Y_SETS).astype(F32), axis=0)
    pre_other = lax.ppermute(pre_mine, "layer", HI_SWAP)
    copies = feature_copies(pre_mine, pre_other, enc_bias[None], gate_rows)
    features = swap_blocks(copies, "layer", Y_SETS).reshape(tokens, feats_here)

    token_start = own_start + chip * per
    stream_rows = lax.dynamic_slice_in_dim(layer_in, token_start, per, 0).astype(F32)
    def middle(slots, features, dec_local):
        slot_ids = lax.iota(jnp.int32, slots)
        slot_mask = slot_here[None, :] == slot_ids[:, None]

        def by_slot(rows):
            spread = rows.reshape(CHIPS, 1, per, feats_here)
            kept = jnp.where(slot_mask[None, :, None, :], spread, jnp.zeros((), BF16))
            return kept.reshape(CHIPS * slots * per, feats_here)

        own_rows = by_slot(lax.dynamic_slice_in_dim(features, own_start, half, 0))
        other_rows = by_slot(lax.dynamic_slice_in_dim(features, other_start, half, 0))
        theirs = jnp.dot(other_rows, dec_local, preferred_element_type=F32).astype(BF16)
        got = lax.ppermute(theirs, "lat", CORE_SWAP).astype(F32)
        ours = jnp.dot(own_rows, dec_local, preferred_element_type=F32)
        chip_sum = (ours + got).astype(BF16).reshape(CHIPS, slots, per, width)
        chip_sum, turned = lax.optimization_barrier((chip_sum, turned_in))
        by_chip = swap_blocks(chip_sum, "lat", PLANE_SETS)
        gram = lax.dot_general(
            turned, turned, (((1,), (1,)), ((), ())), preferred_element_type=F32
        )
        gram = gram + lax.ppermute(gram, "layer", Y_SWAPS[0])
        far_gram = lax.ppermute(gram, "layer", Y_SWAPS[1])
        slot_seg = jnp.minimum(chip_first[:, None] + slot_ids[None, :], groups - 1)
        wanted, loss, gram = owner_step(
            slot_seg, by_chip, stream_rows, dec_bias, gram, far_gram, groups
        )
        own_err = swap_blocks(wanted, "lat", PLANE_SETS).reshape(CHIPS * slots * per, width)
        other_err = lax.ppermute(own_err, "lat", CORE_SWAP)


        def back(err):
            out = lax.dot_general(
                err, dec_local, (((1,), (1,)), ((), ())), preferred_element_type=F32
            ).reshape(CHIPS, slots, per, feats_here)
            kept = jnp.where(slot_mask[None, :, None, :], out, 0.0)
            return jnp.sum(kept, axis=1).astype(BF16).reshape(half, feats_here)

        parts = latent_parts(back(own_err), back(other_err))
        pairs = [
            lax.dot_general(r, r, (((1,), (1,)), ((), ())), preferred_element_type=F32)
            for r in (
                jnp.concatenate([own_rows, other_rows], axis=0),
                jnp.concatenate([own_err, other_err], axis=0),
            )
        ]
        dec_squares = jnp.sum(pairs[0] * pairs[1]).reshape(1, 1)
        return parts, gram, loss, dec_squares

    choices = sorted({min(2, groups), min(3, groups), groups})
    which = sum((slots_needed > c).astype(jnp.int32) for c in choices[:-1])
    parts, gram, loss, dec_squares = lax.switch(
        which, [functools.partial(middle, s) for s in choices], features, dec_local
    )
    mine = jnp.sum(swap_blocks(parts, "layer", Y_SETS).astype(F32), axis=0)
    other = lax.ppermute(mine, "layer", HI_SWAP)
    lanes = lax.broadcasted_iota(jnp.int32, (8, LANES), 1)
    scalars = jnp.where(lanes == 0, dec_squares, jnp.where(lanes == 1, loss, 0.0))
    dpre, rows = dpre_and_rows(
        mine, other, turned_gate, scalars, gram, lat_count * layer_count
    )
    rows = lax.all_to_all(rows, ("lat", "layer"), 0, 0)
    near = jnp.stack([dpre, lax.ppermute(dpre, "layer", Y_SWAPS[0])])
    far = lax.ppermute(near, "layer", Y_SWAPS[1])
    limit = math.sqrt(2.0 * layer_count * width * feats_here * lat_count)
    new_first, new_second, loss_value, grad_norm = update(
        ypos.reshape(1, 1), rows, turned_in, near, far, first_moment[0], second_moment[0],
        limit, 1.0 / (tokens * layer_count * width),
    )
    return (new_first[None], new_second[None], loss_value[0, 0], grad_norm[0, 0])


def solution(mesh):
    in_specs = (
        P(None, "layer", None),
        P("layer", None, "lat"),
        P("lat"),
        P("lat", "layer", None),
        P("layer", None),
        P(None, "lat"),
        P(),
        P("layer", None, "lat"),
        P("layer", None, "lat"),
    )
    out_specs = (P("layer", None, "lat"), P("layer", None, "lat"), P(), P())
    return jax.shard_map(
        on_device, mesh=mesh, in_specs=in_specs, out_specs=out_specs, check_vma=False
    )
```

```python
import functools
import math

import jax
import jax.numpy as jnp
from jax import lax
from jax.experimental import pallas as pl
from jax.experimental.pallas import tpu as pltpu
from jax.sharding import PartitionSpec as P

BF16 = jnp.bfloat16
F32 = jnp.float32

NX, NZ, NCORE, NHI, NY = 4, 4, 2, 2, 4
CHIPS = NX * NZ
PLANE_SETS = [[chip * NCORE + c for chip in range(CHIPS)] for c in range(NCORE)]
Y_SETS = [[h * NY + y for y in range(NY)] for h in range(NHI)]
CORE_SWAP = [(i, i ^ 1) for i in range(CHIPS * NCORE)]
HI_SWAP = [(i, i ^ NY) for i in range(NHI * NY)]
Y_SWAPS = [[(i, i ^ m) for i in range(NHI * NY)] for m in (1, 2)]
LANES = 128
UPDATE_STEPS = 7


def swap_blocks(blocks, axis, sets):
    return lax.all_to_all(blocks, axis, 0, 0, axis_index_groups=sets)


def vmem_specs(count):
    return [pl.BlockSpec(memory_space=pltpu.VMEM)] * count


SMEM_SPEC = pl.BlockSpec(memory_space=pltpu.SMEM)
SMALL = pltpu.CompilerParams(vmem_limit_bytes=10 * 2**20)
LARGE = pltpu.CompilerParams(vmem_limit_bytes=56 * 2**20)


def pre_kernel(in_ref, enc_ref, out_ref, acc):
    step = pl.program_id(0)
    part = jnp.dot(in_ref[...], enc_ref[...], preferred_element_type=F32)

    @pl.when(step == 0)
    def _():
        acc[...] = part

    @pl.when(step > 0)
    def _():
        acc[...] += part

    @pl.when(step == pl.num_programs(0) - 1)
    def _():
        out_ref[...] = acc[...].astype(BF16)


def partial_pre(layer_in, enc):
    tokens, width = layer_in.shape
    feats = enc.shape[1]
    tile = width // 2
    return pl.pallas_call(
        pre_kernel,
        grid=(width // tile,),
        out_shape=jax.ShapeDtypeStruct((tokens, feats), BF16),
        in_specs=[
            pl.BlockSpec((tokens, tile), lambda i: (0, i)),
            pl.BlockSpec((tile, feats), lambda i: (i, 0)),
        ],
        out_specs=pl.BlockSpec((tokens, feats), lambda i: (0, 0)),
        scratch_shapes=[pltpu.VMEM((tokens, feats), F32)],
        compiler_params=LARGE,
    )(layer_in, enc)


def feature_kernel(mine_ref, other_ref, bias_ref, gate_ref, out_ref):
    pre = mine_ref[...].astype(F32) + other_ref[...].astype(F32) + bias_ref[...]
    features = (pre * gate_ref[...]).astype(BF16)
    for y in range(NY):
        out_ref[y] = features


def feature_copies(mine, other, bias, gate):
    return pl.pallas_call(
        feature_kernel,
        out_shape=jax.ShapeDtypeStruct((NY, *mine.shape), BF16),
        in_specs=vmem_specs(4),
        out_specs=vmem_specs(1)[0],
        compiler_params=SMALL,
    )(mine, other, bias, gate)


def parts_kernel(own_ref, other_ref, out_ref):
    half, feats = own_ref.shape
    block = feats // NY
    for y in range(NY):
        out_ref[y, 0:half, :] = own_ref[:, y * block : (y + 1) * block]
        out_ref[y, half : 2 * half, :] = other_ref[:, y * block : (y + 1) * block]


def latent_parts(own, other):
    half, feats = own.shape
    return pl.pallas_call(
        parts_kernel,
        out_shape=jax.ShapeDtypeStruct((NY, NCORE * half, feats // NY), BF16),
        in_specs=vmem_specs(2),
        out_specs=vmem_specs(1)[0],
        compiler_params=SMALL,
    )(own, other)


def dpre_kernel(
    mine_ref, other_ref, gate_ref, scalars_ref, gram_hbm, out_ref, rows_ref, gram, sem
):
    copy = pltpu.make_async_copy(gram_hbm, gram, sem)
    copy.start()
    dfeat = mine_ref[...].astype(F32) + other_ref[...].astype(F32)
    dpre = (dfeat * gate_ref[...]).astype(BF16)
    out_ref[...] = dpre
    pairs = lax.dot_general(dpre, dpre, (((1,), (1,)), ((), ())), preferred_element_type=F32)
    copy.wait()
    squares = jnp.sum(pairs * gram[...])
    lanes = lax.broadcasted_iota(jnp.int32, (1, LANES), 1)
    row = scalars_ref[0:1, :] + jnp.where(lanes == 0, squares, 0.0)
    rows_ref[...] = jnp.broadcast_to(row[None], rows_ref.shape)


def dpre_and_rows(mine, other, gate, scalars, gram, devices):
    return pl.pallas_call(
        dpre_kernel,
        out_shape=(
            jax.ShapeDtypeStruct(mine.shape, BF16),
            jax.ShapeDtypeStruct((devices, 1, LANES), F32),
        ),
        in_specs=vmem_specs(4) + [pl.BlockSpec(memory_space=pl.ANY)],
        out_specs=vmem_specs(2),
        scratch_shapes=[pltpu.VMEM(gram.shape, F32), pltpu.SemaphoreType.DMA],
        compiler_params=SMALL,
    )(mine, other, gate, scalars, gram)


def owner_kernel(
    slots, groups, seg_ref, got_ref, rows_ref, bias_ref, near_ref, far_ref,
    out_ref, loss_ref, gram_hbm, sums, errs, gram, sem,
):
    gram[...] = near_ref[...] + far_ref[...]
    copy = pltpu.make_async_copy(gram, gram_hbm, sem)
    copy.start()
    sums[...] = jnp.zeros_like(sums)
    for c in range(CHIPS):
        for e in range(slots):
            s = seg_ref[c, e]
            sums[s] += got_ref[c, e].astype(F32)
    recon = jnp.zeros_like(rows_ref)
    loss = jnp.zeros_like(rows_ref)
    grad_err = []
    for k in range(groups):
        recon += sums[k]
        residual = recon + bias_ref[...] - rows_ref[...]
        loss += residual * residual
        grad_err.append((2.0 * residual).astype(BF16).astype(F32))
    total = jnp.zeros_like(rows_ref)
    for k in range(groups - 1, -1, -1):
        total += grad_err[k]
        errs[k] = total.astype(BF16)
    loss_ref[0, 0] = jnp.sum(loss)
    for c in range(CHIPS):
        for e in range(slots):
            out_ref[c, e] = errs[seg_ref[c, e]]
    copy.wait()


def owner_step(slot_seg, got, rows, bias, near_gram, far_gram, groups):
    chips, slots, per, width = got.shape
    vmem = pl.BlockSpec(memory_space=pltpu.VMEM)
    smem = pl.BlockSpec(memory_space=pltpu.SMEM)
    return pl.pallas_call(
        functools.partial(owner_kernel, slots, groups),
        out_shape=(
            jax.ShapeDtypeStruct(got.shape, BF16),
            jax.ShapeDtypeStruct((1, 1), F32),
            jax.ShapeDtypeStruct(near_gram.shape, F32),
        ),
        in_specs=[smem, vmem, vmem, vmem, vmem, vmem],
        out_specs=(vmem, smem, pl.BlockSpec(memory_space=pl.ANY)),
        scratch_shapes=[
            pltpu.VMEM((groups, per, width), F32),
            pltpu.VMEM((groups, per, width), BF16),
            pltpu.VMEM(near_gram.shape, F32),
            pltpu.SemaphoreType.DMA,
        ],
        compiler_params=SMALL,
    )(slot_seg, got, rows, bias, near_gram, far_gram)


def update_kernel(
    limit, loss_scale, ypos_ref, rows_ref, in_ref, near_ref, far_ref, first, second,
    new_first_hbm, new_second_hbm, loss_ref, norm_ref,
    dpre, new_first, new_second, sems,
):
    width = in_ref.shape[1]
    tile = width // UPDATE_STEPS
    block = near_ref.shape[2]
    for at, ref in ((0, near_ref), (2, far_ref)):
        for b in range(2):
            owner = ypos_ref[0, 0] ^ (at + b)
            dpre[:, pl.ds(pl.multiple_of(owner * block, block), block)] = ref[b]
    totals = jnp.sum(rows_ref[...], axis=0)
    lanes = lax.broadcasted_iota(jnp.int32, totals.shape, 1)
    squares = jnp.sum(jnp.where(lanes == 0, totals, 0.0), axis=1, keepdims=True)
    loss = jnp.sum(jnp.where(lanes == 1, totals, 0.0), axis=1, keepdims=True)
    norm = jnp.sqrt(squares)
    factor = limit / jnp.maximum(norm, limit)
    loss_ref[...] = loss * loss_scale
    norm_ref[...] = norm
    copies = []
    for i in range(UPDATE_STEPS):
        here = slice(i * tile, (i + 1) * tile)
        rows = pl.ds(i * tile, tile)
        grad = lax.dot_general(
            in_ref[:, here], dpre[...], (((0,), (0,)), ((), ())), preferred_element_type=F32
        )
        clipped = factor * grad
        new_first[here, :] = (0.9 * first[here, :].astype(F32) + 0.1 * clipped).astype(BF16)
        new_second[here, :] = (
            0.95 * second[here, :].astype(F32) + 0.05 * clipped * clipped
        ).astype(BF16)
        for n, (src, dst) in enumerate(
            ((new_first, new_first_hbm), (new_second, new_second_hbm))
        ):
            copy = pltpu.make_async_copy(src.at[rows, :], dst.at[rows, :], sems.at[n, i])
            copy.start()
            copies.append(copy)
    for copy in copies:
        copy.wait()


def update(ypos, rows, layer_in, near, far, first, second, limit, loss_scale):
    width, feats = first.shape
    tokens = layer_in.shape[0]
    hbm = pl.BlockSpec(memory_space=pl.ANY)
    whole = pltpu.VMEM((width, feats), BF16)
    return pl.pallas_call(
        functools.partial(update_kernel, limit, loss_scale),
        out_shape=(jax.ShapeDtypeStruct((width, feats), BF16),) * 2
        + (jax.ShapeDtypeStruct((1, 1), F32),) * 2,
        in_specs=[SMEM_SPEC] + vmem_specs(6),
        out_specs=[hbm] * 2 + vmem_specs(2),
        scratch_shapes=[
            pltpu.VMEM((tokens, feats), BF16), whole, whole,
            pltpu.SemaphoreType.DMA((2, UPDATE_STEPS)),
        ],
        compiler_params=pltpu.CompilerParams(vmem_limit_bytes=13 * 2**20),
    )(ypos, rows, layer_in, near, far, first, second)


def on_device(
    streams, enc_weight, enc_bias, dec_weight, dec_bias, active, bounds, first_moment, second_moment
):
    lat_count = lax.axis_size("lat")
    layer_count = lax.axis_size("layer")
    lat = lax.axis_index("lat")
    layer = lax.axis_index("layer")
    tokens = streams.shape[0]
    width = streams.shape[2]
    feats_here = enc_weight.shape[2]
    groups = bounds.shape[0]
    core, chip = lat % NCORE, lat // NCORE
    ypos = layer % NY
    half = tokens // NCORE
    per = half // CHIPS
    quarter = tokens // NY
    layer_in = streams[:, 0, :]
    enc_local = enc_weight[0]
    dec_local = dec_weight[:, 0, :]

    own_start, other_start = core * half, (1 - core) * half
    own_in = lax.dynamic_slice_in_dim(layer_in, own_start, half, 0)
    other_in = lax.dynamic_slice_in_dim(layer_in, other_start, half, 0)
    turned_in = jnp.concatenate([own_in, other_in], axis=0)
    gate = active.astype(F32)
    gate_rows = lax.dynamic_slice_in_dim(gate, ypos * quarter, quarter, 0)
    gate_cols = lax.dynamic_slice_in_dim(gate, ypos * (feats_here // NY), feats_here // NY, 1)
    turned_gate = jnp.concatenate(
        [
            lax.dynamic_slice_in_dim(gate_cols, own_start, half, 0),
            lax.dynamic_slice_in_dim(gate_cols, other_start, half, 0),
        ],
        axis=0,
    )

    latent_ids = lat * feats_here + lax.iota(jnp.int32, feats_here)
    seg = jnp.sum((bounds[:, None] <= latent_ids[None, :]).astype(jnp.int32), axis=0)
    chip_feats = NCORE * feats_here
    chip_starts = lax.iota(jnp.int32, CHIPS) * chip_feats
    chip_first = jnp.sum((bounds[None, :] <= chip_starts[:, None]).astype(jnp.int32), axis=1)
    chip_last = jnp.sum(
        (bounds[None, :] <= chip_starts[:, None] + (chip_feats - 1)).astype(jnp.int32), axis=1
    )
    slots_needed = jnp.max(chip_last - chip_first) + 1
    first_here = lax.dynamic_index_in_dim(chip_first, chip, 0, keepdims=False)
    slot_here = lax.optimization_barrier(seg - first_here)

    pre_parts = partial_pre(layer_in, enc_local).reshape(NY, quarter, feats_here)
    pre_mine = jnp.sum(swap_blocks(pre_parts, "layer", Y_SETS).astype(F32), axis=0).astype(BF16)
    pre_other = lax.ppermute(pre_mine, "layer", HI_SWAP)
    copies = feature_copies(pre_mine, pre_other, enc_bias[None], gate_rows)
    features = swap_blocks(copies, "layer", Y_SETS).reshape(tokens, feats_here)

    token_start = own_start + chip * per
    stream_rows = lax.dynamic_slice_in_dim(layer_in, token_start, per, 0).astype(F32)
    def middle(slots, features, dec_local):
        slot_ids = lax.iota(jnp.int32, slots)
        slot_mask = slot_here[None, :] == slot_ids[:, None]

        def by_slot(rows):
            spread = rows.reshape(CHIPS, 1, per, feats_here)
            kept = jnp.where(slot_mask[None, :, None, :], spread, jnp.zeros((), BF16))
            return kept.reshape(CHIPS * slots * per, feats_here)

        own_rows = by_slot(lax.dynamic_slice_in_dim(features, own_start, half, 0))
        other_rows = by_slot(lax.dynamic_slice_in_dim(features, other_start, half, 0))
        theirs = jnp.dot(other_rows, dec_local, preferred_element_type=F32).astype(BF16)
        got = lax.ppermute(theirs, "lat", CORE_SWAP).astype(F32)
        ours = jnp.dot(own_rows, dec_local, preferred_element_type=F32)
        chip_sum = (ours + got).astype(BF16).reshape(CHIPS, slots, per, width)
        chip_sum, turned = lax.optimization_barrier((chip_sum, turned_in))
        by_chip = swap_blocks(chip_sum, "lat", PLANE_SETS)
        gram = lax.dot_general(
            turned, turned, (((1,), (1,)), ((), ())), preferred_element_type=F32
        )
        gram = gram + lax.ppermute(gram, "layer", Y_SWAPS[0])
        far_gram = lax.ppermute(gram, "layer", Y_SWAPS[1])
        slot_seg = jnp.minimum(chip_first[:, None] + slot_ids[None, :], groups - 1)
        wanted, loss, gram = owner_step(
            slot_seg, by_chip, stream_rows, dec_bias, gram, far_gram, groups
        )
        own_err = swap_blocks(wanted, "lat", PLANE_SETS).reshape(CHIPS * slots * per, width)
        other_err = lax.ppermute(own_err, "lat", CORE_SWAP)


        def back(err):
            out = lax.dot_general(
                err, dec_local, (((1,), (1,)), ((), ())), preferred_element_type=F32
            ).reshape(CHIPS, slots, per, feats_here)
            kept = jnp.where(slot_mask[None, :, None, :], out, 0.0)
            return jnp.sum(kept, axis=1).astype(BF16).reshape(half, feats_here)

        parts = latent_parts(back(own_err), back(other_err))
        pairs = [
            lax.dot_general(r, r, (((1,), (1,)), ((), ())), preferred_element_type=F32)
            for r in (
                jnp.concatenate([own_rows, other_rows], axis=0),
                jnp.concatenate([own_err, other_err], axis=0),
            )
        ]
        dec_squares = jnp.sum(pairs[0] * pairs[1]).reshape(1, 1)
        return parts, gram, loss, dec_squares

    choices = sorted({min(2, groups), min(3, groups), groups})
    which = sum((slots_needed > c).astype(jnp.int32) for c in choices[:-1])
    parts, gram, loss, dec_squares = lax.switch(
        which, [functools.partial(middle, s) for s in choices], features, dec_local
    )
    mine = jnp.sum(swap_blocks(parts, "layer", Y_SETS).astype(F32), axis=0).astype(BF16)
    other = lax.ppermute(mine, "layer", HI_SWAP)
    lanes = lax.broadcasted_iota(jnp.int32, (8, LANES), 1)
    scalars = jnp.where(lanes == 0, dec_squares, jnp.where(lanes == 1, loss, 0.0))
    dpre, rows = dpre_and_rows(
        mine, other, turned_gate, scalars, gram, lat_count * layer_count
    )
    rows = lax.all_to_all(rows, ("lat", "layer"), 0, 0)
    near = jnp.stack([dpre, lax.ppermute(dpre, "layer", Y_SWAPS[0])])
    far = lax.ppermute(near, "layer", Y_SWAPS[1])
    limit = math.sqrt(2.0 * layer_count * width * feats_here * lat_count)
    new_first, new_second, loss_value, grad_norm = update(
        ypos.reshape(1, 1), rows, turned_in, near, far, first_moment[0], second_moment[0],
        limit, 1.0 / (tokens * layer_count * width),
    )
    return (new_first[None], new_second[None], loss_value[0, 0], grad_norm[0, 0])


def solution(mesh):
    in_specs = (
        P(None, "layer", None),
        P("layer", None, "lat"),
        P("lat"),
        P("lat", "layer", None),
        P("layer", None),
        P(None, "lat"),
        P(),
        P("layer", None, "lat"),
        P("layer", None, "lat"),
    )
    out_specs = (P("layer", None, "lat"), P("layer", None, "lat"), P(), P())
    return jax.shard_map(
        on_device, mesh=mesh, in_specs=in_specs, out_specs=out_specs, check_vma=False
    )
```

```python
import functools
import math

import jax
import jax.numpy as jnp
from jax import lax
from jax.experimental import pallas as pl
from jax.experimental.pallas import tpu as pltpu
from jax.sharding import PartitionSpec as P

BF16 = jnp.bfloat16
F32 = jnp.float32

NX, NZ, NCORE, NHI, NY = 4, 4, 2, 2, 4
CHIPS = NX * NZ
PLANE_SETS = [[chip * NCORE + c for chip in range(CHIPS)] for c in range(NCORE)]
Y_SETS = [[h * NY + y for y in range(NY)] for h in range(NHI)]
CORE_SWAP = [(i, i ^ 1) for i in range(CHIPS * NCORE)]
HI_SWAP = [(i, i ^ NY) for i in range(NHI * NY)]
Y_SWAPS = [[(i, i ^ m) for i in range(NHI * NY)] for m in (1, 2)]
LANES = 128
UPDATE_STEPS = 7


def swap_blocks(blocks, axis, sets):
    return lax.all_to_all(blocks, axis, 0, 0, axis_index_groups=sets)


def vmem_specs(count):
    return [pl.BlockSpec(memory_space=pltpu.VMEM)] * count


SMALL = pltpu.CompilerParams(vmem_limit_bytes=10 * 2**20)
LARGE = pltpu.CompilerParams(vmem_limit_bytes=56 * 2**20)


def pre_kernel(in_ref, enc_ref, out_ref, acc):
    step = pl.program_id(0)
    part = jnp.dot(in_ref[...], enc_ref[...], preferred_element_type=F32)

    @pl.when(step == 0)
    def _():
        acc[...] = part

    @pl.when(step > 0)
    def _():
        acc[...] += part

    @pl.when(step == pl.num_programs(0) - 1)
    def _():
        out_ref[...] = acc[...].astype(BF16)


def partial_pre(layer_in, enc):
    tokens, width = layer_in.shape
    feats = enc.shape[1]
    tile = width // 2
    return pl.pallas_call(
        pre_kernel,
        grid=(width // tile,),
        out_shape=jax.ShapeDtypeStruct((tokens, feats), BF16),
        in_specs=[
            pl.BlockSpec((tokens, tile), lambda i: (0, i)),
            pl.BlockSpec((tile, feats), lambda i: (i, 0)),
        ],
        out_specs=pl.BlockSpec((tokens, feats), lambda i: (0, 0)),
        scratch_shapes=[pltpu.VMEM((tokens, feats), F32)],
        compiler_params=LARGE,
    )(layer_in, enc)


def feature_kernel(mine_ref, other_ref, bias_ref, gate_ref, out_ref):
    pre = mine_ref[...].astype(F32) + other_ref[...].astype(F32) + bias_ref[...]
    features = (pre * gate_ref[...]).astype(BF16)
    for y in range(NY):
        out_ref[y] = features


def feature_copies(mine, other, bias, gate):
    return pl.pallas_call(
        feature_kernel,
        out_shape=jax.ShapeDtypeStruct((NY, *mine.shape), BF16),
        in_specs=vmem_specs(4),
        out_specs=vmem_specs(1)[0],
        compiler_params=SMALL,
    )(mine, other, bias, gate)


def parts_kernel(own_ref, other_ref, out_ref):
    half, feats = own_ref.shape
    block = feats // NY
    for y in range(NY):
        out_ref[y, 0:half, :] = own_ref[:, y * block : (y + 1) * block]
        out_ref[y, half : 2 * half, :] = other_ref[:, y * block : (y + 1) * block]


def latent_parts(own, other):
    half, feats = own.shape
    return pl.pallas_call(
        parts_kernel,
        out_shape=jax.ShapeDtypeStruct((NY, NCORE * half, feats // NY), BF16),
        in_specs=vmem_specs(2),
        out_specs=vmem_specs(1)[0],
        compiler_params=SMALL,
    )(own, other)


def dpre_kernel(
    mine_ref, other_ref, gate_ref, scalars_ref, gram_hbm, out_ref, rows_ref, gram, sem
):
    copy = pltpu.make_async_copy(gram_hbm, gram, sem)
    copy.start()
    dfeat = mine_ref[...].astype(F32) + other_ref[...].astype(F32)
    dpre = (dfeat * gate_ref[...]).astype(BF16)
    out_ref[...] = dpre
    pairs = lax.dot_general(dpre, dpre, (((1,), (1,)), ((), ())), preferred_element_type=F32)
    copy.wait()
    squares = jnp.sum(pairs * gram[...])
    lanes = lax.broadcasted_iota(jnp.int32, (1, LANES), 1)
    row = scalars_ref[0:1, :] + jnp.where(lanes == 0, squares, 0.0)
    rows_ref[...] = jnp.broadcast_to(row[None], rows_ref.shape)


def dpre_and_rows(mine, other, gate, scalars, gram, devices):
    return pl.pallas_call(
        dpre_kernel,
        out_shape=(
            jax.ShapeDtypeStruct(mine.shape, BF16),
            jax.ShapeDtypeStruct((devices, 1, LANES), F32),
        ),
        in_specs=vmem_specs(4) + [pl.BlockSpec(memory_space=pl.ANY)],
        out_specs=vmem_specs(2),
        scratch_shapes=[pltpu.VMEM(gram.shape, F32), pltpu.SemaphoreType.DMA],
        compiler_params=SMALL,
    )(mine, other, gate, scalars, gram)


def owner_kernel(
    slots, groups, seg_ref, got_ref, rows_ref, bias_ref, near_ref, far_ref,
    out_ref, loss_ref, gram_hbm, sums, errs, gram, sem,
):
    gram[...] = near_ref[...] + far_ref[...]
    copy = pltpu.make_async_copy(gram, gram_hbm, sem)
    copy.start()
    sums[...] = jnp.zeros_like(sums)
    for c in range(CHIPS):
        for e in range(slots):
            s = seg_ref[c, e]
            sums[s] += got_ref[c, e].astype(F32)
    recon = jnp.zeros_like(rows_ref)
    loss = jnp.zeros_like(rows_ref)
    grad_err = []
    for k in range(groups):
        recon += sums[k]
        residual = recon + bias_ref[...] - rows_ref[...]
        loss += residual * residual
        grad_err.append((2.0 * residual).astype(BF16).astype(F32))
    total = jnp.zeros_like(rows_ref)
    for k in range(groups - 1, -1, -1):
        total += grad_err[k]
        errs[k] = total.astype(BF16)
    loss_ref[0, 0] = jnp.sum(loss)
    for c in range(CHIPS):
        for e in range(slots):
            out_ref[c, e] = errs[seg_ref[c, e]]
    copy.wait()


def owner_step(slot_seg, got, rows, bias, near_gram, far_gram, groups):
    chips, slots, per, width = got.shape
    vmem = pl.BlockSpec(memory_space=pltpu.VMEM)
    smem = pl.BlockSpec(memory_space=pltpu.SMEM)
    return pl.pallas_call(
        functools.partial(owner_kernel, slots, groups),
        out_shape=(
            jax.ShapeDtypeStruct(got.shape, BF16),
            jax.ShapeDtypeStruct((1, 1), F32),
            jax.ShapeDtypeStruct(near_gram.shape, F32),
        ),
        in_specs=[smem, vmem, vmem, vmem, vmem, vmem],
        out_specs=(vmem, smem, pl.BlockSpec(memory_space=pl.ANY)),
        scratch_shapes=[
            pltpu.VMEM((groups, per, width), F32),
            pltpu.VMEM((groups, per, width), BF16),
            pltpu.VMEM(near_gram.shape, F32),
            pltpu.SemaphoreType.DMA,
        ],
        compiler_params=SMALL,
    )(slot_seg, got, rows, bias, near_gram, far_gram)


def update_kernel(
    limit, loss_scale, rows_ref, in_ref, near_ref, far_ref, first, second,
    new_first_hbm, new_second_hbm, loss_ref, norm_ref,
    dpre, new_first, new_second, sems,
):
    width = in_ref.shape[1]
    tile = width // UPDATE_STEPS
    block = near_ref.shape[2]
    ypos = lax.axis_index("layer") % NY
    for at, ref in ((0, near_ref), (2, far_ref)):
        for b in range(2):
            owner = ypos ^ (at + b)
            dpre[:, pl.ds(pl.multiple_of(owner * block, block), block)] = ref[b]
    totals = jnp.sum(rows_ref[...], axis=0)
    lanes = lax.broadcasted_iota(jnp.int32, totals.shape, 1)
    squares = jnp.sum(jnp.where(lanes == 0, totals, 0.0), axis=1, keepdims=True)
    loss = jnp.sum(jnp.where(lanes == 1, totals, 0.0), axis=1, keepdims=True)
    norm = jnp.sqrt(squares)
    factor = limit / jnp.maximum(norm, limit)
    loss_ref[...] = loss * loss_scale
    norm_ref[...] = norm
    copies = []
    for i in range(UPDATE_STEPS):
        here = slice(i * tile, (i + 1) * tile)
        rows = pl.ds(i * tile, tile)
        grad = lax.dot_general(
            in_ref[:, here], dpre[...], (((0,), (0,)), ((), ())), preferred_element_type=F32
        )
        clipped = factor * grad
        new_first[here, :] = (0.9 * first[here, :].astype(F32) + 0.1 * clipped).astype(BF16)
        new_second[here, :] = (
            0.95 * second[here, :].astype(F32) + 0.05 * clipped * clipped
        ).astype(BF16)
        for n, (src, dst) in enumerate(
            ((new_first, new_first_hbm), (new_second, new_second_hbm))
        ):
            copy = pltpu.make_async_copy(src.at[rows, :], dst.at[rows, :], sems.at[n, i])
            copy.start()
            copies.append(copy)
    for copy in copies:
        copy.wait()


def update(rows, layer_in, near, far, first, second, limit, loss_scale):
    width, feats = first.shape
    tokens = layer_in.shape[0]
    hbm = pl.BlockSpec(memory_space=pl.ANY)
    whole = pltpu.VMEM((width, feats), BF16)
    return pl.pallas_call(
        functools.partial(update_kernel, limit, loss_scale),
        out_shape=(jax.ShapeDtypeStruct((width, feats), BF16),) * 2
        + (jax.ShapeDtypeStruct((1, 1), F32),) * 2,
        in_specs=vmem_specs(6),
        out_specs=[hbm] * 2 + vmem_specs(2),
        scratch_shapes=[
            pltpu.VMEM((tokens, feats), BF16), whole, whole,
            pltpu.SemaphoreType.DMA((2, UPDATE_STEPS)),
        ],
        compiler_params=pltpu.CompilerParams(vmem_limit_bytes=13 * 2**20),
    )(rows, layer_in, near, far, first, second)


def on_device(
    streams, enc_weight, enc_bias, dec_weight, dec_bias, active, bounds, first_moment, second_moment
):
    lat_count = lax.axis_size("lat")
    layer_count = lax.axis_size("layer")
    lat = lax.axis_index("lat")
    layer = lax.axis_index("layer")
    tokens = streams.shape[0]
    width = streams.shape[2]
    feats_here = enc_weight.shape[2]
    groups = bounds.shape[0]
    core, chip = lat % NCORE, lat // NCORE
    ypos = layer % NY
    half = tokens // NCORE
    per = half // CHIPS
    quarter = tokens // NY
    layer_in = streams[:, 0, :]
    enc_local = enc_weight[0]
    dec_local = dec_weight[:, 0, :]

    own_start, other_start = core * half, (1 - core) * half
    own_in = lax.dynamic_slice_in_dim(layer_in, own_start, half, 0)
    other_in = lax.dynamic_slice_in_dim(layer_in, other_start, half, 0)
    turned_in = jnp.concatenate([own_in, other_in], axis=0)
    gate = active.astype(F32)
    gate_rows = lax.dynamic_slice_in_dim(gate, ypos * quarter, quarter, 0)
    gate_cols = lax.dynamic_slice_in_dim(gate, ypos * (feats_here // NY), feats_here // NY, 1)
    turned_gate = jnp.concatenate(
        [
            lax.dynamic_slice_in_dim(gate_cols, own_start, half, 0),
            lax.dynamic_slice_in_dim(gate_cols, other_start, half, 0),
        ],
        axis=0,
    )

    latent_ids = lat * feats_here + lax.iota(jnp.int32, feats_here)
    seg = jnp.sum((bounds[:, None] <= latent_ids[None, :]).astype(jnp.int32), axis=0)
    chip_feats = NCORE * feats_here
    chip_starts = lax.iota(jnp.int32, CHIPS) * chip_feats
    chip_first = jnp.sum((bounds[None, :] <= chip_starts[:, None]).astype(jnp.int32), axis=1)
    chip_last = jnp.sum(
        (bounds[None, :] <= chip_starts[:, None] + (chip_feats - 1)).astype(jnp.int32), axis=1
    )
    slots_needed = jnp.max(chip_last - chip_first) + 1
    first_here = lax.dynamic_index_in_dim(chip_first, chip, 0, keepdims=False)
    slot_here = lax.optimization_barrier(seg - first_here)

    pre_parts = partial_pre(layer_in, enc_local).reshape(NY, quarter, feats_here)
    pre_mine = jnp.sum(swap_blocks(pre_parts, "layer", Y_SETS).astype(F32), axis=0).astype(BF16)
    pre_other = lax.ppermute(pre_mine, "layer", HI_SWAP)
    copies = feature_copies(pre_mine, pre_other, enc_bias[None], gate_rows)
    features = swap_blocks(copies, "layer", Y_SETS).reshape(tokens, feats_here)

    token_start = own_start + chip * per
    stream_rows = lax.dynamic_slice_in_dim(layer_in, token_start, per, 0).astype(F32)
    def middle(slots, features, dec_local):
        slot_ids = lax.iota(jnp.int32, slots)
        slot_mask = slot_here[None, :] == slot_ids[:, None]

        def by_slot(rows):
            spread = rows.reshape(CHIPS, 1, per, feats_here)
            kept = jnp.where(slot_mask[None, :, None, :], spread, jnp.zeros((), BF16))
            return kept.reshape(CHIPS * slots * per, feats_here)

        own_rows = by_slot(lax.dynamic_slice_in_dim(features, own_start, half, 0))
        other_rows = by_slot(lax.dynamic_slice_in_dim(features, other_start, half, 0))
        theirs = jnp.dot(other_rows, dec_local, preferred_element_type=F32).astype(BF16)
        got = lax.ppermute(theirs, "lat", CORE_SWAP).astype(F32)
        ours = jnp.dot(own_rows, dec_local, preferred_element_type=F32)
        chip_sum = (ours + got).astype(BF16).reshape(CHIPS, slots, per, width)
        chip_sum, turned = lax.optimization_barrier((chip_sum, turned_in))
        by_chip = swap_blocks(chip_sum, "lat", PLANE_SETS)
        gram = lax.dot_general(
            turned, turned, (((1,), (1,)), ((), ())), preferred_element_type=F32
        )
        gram = gram + lax.ppermute(gram, "layer", Y_SWAPS[0])
        far_gram = lax.ppermute(gram, "layer", Y_SWAPS[1])
        slot_seg = jnp.minimum(chip_first[:, None] + slot_ids[None, :], groups - 1)
        wanted, loss, gram = owner_step(
            slot_seg, by_chip, stream_rows, dec_bias, gram, far_gram, groups
        )
        own_err = swap_blocks(wanted, "lat", PLANE_SETS).reshape(CHIPS * slots * per, width)
        other_err = lax.ppermute(own_err, "lat", CORE_SWAP)


        def back(err):
            out = lax.dot_general(
                err, dec_local, (((1,), (1,)), ((), ())), preferred_element_type=F32
            ).reshape(CHIPS, slots, per, feats_here)
            kept = jnp.where(slot_mask[None, :, None, :], out, 0.0)
            return jnp.sum(kept, axis=1).astype(BF16).reshape(half, feats_here)

        parts = latent_parts(back(own_err), back(other_err))
        pairs = [
            lax.dot_general(r, r, (((1,), (1,)), ((), ())), preferred_element_type=F32)
            for r in (
                jnp.concatenate([own_rows, other_rows], axis=0),
                jnp.concatenate([own_err, other_err], axis=0),
            )
        ]
        dec_squares = jnp.sum(pairs[0] * pairs[1]).reshape(1, 1)
        return parts, gram, loss, dec_squares

    choices = sorted({min(2, groups), min(3, groups), groups})
    which = sum((slots_needed > c).astype(jnp.int32) for c in choices[:-1])
    parts, gram, loss, dec_squares = lax.switch(
        which, [functools.partial(middle, s) for s in choices], features, dec_local
    )
    mine = jnp.sum(swap_blocks(parts, "layer", Y_SETS).astype(F32), axis=0).astype(BF16)
    other = lax.ppermute(mine, "layer", HI_SWAP)
    lanes = lax.broadcasted_iota(jnp.int32, (8, LANES), 1)
    scalars = jnp.where(lanes == 0, dec_squares, jnp.where(lanes == 1, loss, 0.0))
    dpre, rows = dpre_and_rows(
        mine, other, turned_gate, scalars, gram, lat_count * layer_count
    )
    rows = lax.all_to_all(rows, ("lat", "layer"), 0, 0)
    near = jnp.stack([dpre, lax.ppermute(dpre, "layer", Y_SWAPS[0])])
    far = lax.ppermute(near, "layer", Y_SWAPS[1])
    limit = math.sqrt(2.0 * layer_count * width * feats_here * lat_count)
    new_first, new_second, loss_value, grad_norm = update(
        rows, turned_in, near, far, first_moment[0], second_moment[0],
        limit, 1.0 / (tokens * layer_count * width),
    )
    return (new_first[None], new_second[None], loss_value[0, 0], grad_norm[0, 0])


def solution(mesh):
    in_specs = (
        P(None, "layer", None),
        P("layer", None, "lat"),
        P("lat"),
        P("lat", "layer", None),
        P("layer", None),
        P(None, "lat"),
        P(),
        P("layer", None, "lat"),
        P("layer", None, "lat"),
    )
    out_specs = (P("layer", None, "lat"), P("layer", None, "lat"), P(), P())
    return jax.shard_map(
        on_device, mesh=mesh, in_specs=in_specs, out_specs=out_specs, check_vma=False
    )
```
